32 devices in a mesh: seq: 8 (over y, x, core), fsdp: 4 (over z).
Axes of the slice: x: 2, y: 2, z: 4, core: 2. Of those that a mesh axis runs over, the one named last changes fastest.
Arguments:
- inputs: bfloat16 [4, 1024, 768], P('fsdp', 'seq'), may hold values from -6 to 6
- positions: int32 [4, 1024], P('fsdp', 'seq'), may hold values from 0 to 1023, as said below
- cotangent: bfloat16 [4, 1024, 768], P('fsdp', 'seq'), may hold values from -6 to 6
- w_qkv: bfloat16 [768, 2304], P('fsdp'), may hold values from -0.21875 to 0.21875
- w_out: bfloat16 [768, 768], P('fsdp'), may hold values from -0.875 to 0.875
- w_in: bfloat16 [768, 2304], P('fsdp'), may hold values from -0.21875 to 0.21875
- w_down: bfloat16 [1152, 768], P('fsdp'), may hold values from -0.1875 to 0.1875
- gain_attn: bfloat16 [768], P('fsdp'), may hold values from 0.5 to 1.5
- gain_mlp: bfloat16 [768], P('fsdp'), may hold values from 0.5 to 1.5
Outputs:
- output: bfloat16 [4, 1024, 768], P('fsdp', 'seq')
- grad_inputs: float32 [4, 1024, 768], P('fsdp', 'seq')
- grad_qkv: float32 [768, 2304], P('fsdp')
- grad_out: float32 [768, 768], P('fsdp')
- grad_in: float32 [768, 2304], P('fsdp')
- grad_down: float32 [1152, 768], P('fsdp')
- grad_gain_attn: float32 [768], P('fsdp')
- grad_gain_mlp: float32 [768], P('fsdp')
The draws below stay inside these ranges and needn't reach their ends.
Inputs may be any that keep to these rules, and one draw needn't show every extreme that they name: `positions`: positions restart at 0 at each sequence start and otherwise rise by one from token to token; the stream's first sequence may begin at a position above 0. No sequence is longer than 8192 tokens. One sequence of each stream begins within its first 128 tokens and ends within its last 128. The first stream reaches the largest position.
All inputs are finite; a program needn't handle non-finite values.
Results may differ from the reference program's by a relative error of at most 0.018.
Values may be sent and summed in bfloat16 or wider, within the bound.
A program may use at most 128 MiB of HBM per device.

```python
import jax
import jax.numpy as jnp
from jax import lax

D = 768
HEADS = 12
HEAD_DIM = 64
FF = 1152
HALF_WINDOW = 64
TOK_DEV = 128
STREAMS = 4
STREAM_LEN = 1024


def draw_positions(key, part):
    key = jax.random.fold_in(key, 7)
    first_key, last_key, offset_key = jax.random.split(key, 3)
    first = jax.random.randint(first_key, (STREAMS, 1), 1, TOK_DEV)
    last = jax.random.randint(last_key, (STREAMS, 1), STREAM_LEN - TOK_DEV + 1, STREAM_LEN)
    offset = jax.random.randint(offset_key, (STREAMS, 1), 0, STREAM_LEN - TOK_DEV)
    stream_index = jnp.arange(STREAMS, dtype=jnp.int32)[:, None]
    offset = jnp.where(stream_index == 0, STREAM_LEN - first, offset)
    index = jnp.arange(STREAM_LEN, dtype=jnp.int32)[None, :]
    start = jnp.where(index >= last, last, jnp.where(index >= first, first, -offset))
    return (index - start).astype(jnp.int32)


def level_of(key, shape, shards, low, top_value):
    loudness = 1.0
    for position, parts in shards:
        draws = jax.random.uniform(jax.random.fold_in(jax.random.fold_in(key, 6), position), (parts,), jnp.float32, low / len(shards), top_value / len(shards))
        loudness = loudness * jnp.repeat(jnp.exp(draws), shape[position] // parts).reshape((-1,) + (1,) * (len(shape) - 1 - position))
    return loudness


def gaussian(own_key, shape, scale, bound, cuts=(), kind=jnp.bfloat16):
    values = jax.random.normal(own_key, shape, jnp.float32) * scale
    if len(cuts) > 0:
        values = level_of(own_key, shape, cuts, -0.22, 0.18) * values
    return jnp.clip(values, min=-bound, max=bound).astype(kind)


def setup_inputs(seed: int = 0) -> dict:
    splits = jax.random.split(jax.random.key(seed), 10)
    inputs = gaussian(splits[0], (STREAMS, STREAM_LEN, D), 1.0, 6.0, ((0, 4), (1, 8)))
    positions = draw_positions(jax.random.fold_in(splits[9], 71), 0)
    cotangent = gaussian(splits[2], (STREAMS, STREAM_LEN, D), 1.0, 6.0, ((0, 4), (1, 8)))
    w_qkv = gaussian(splits[3], (D, 3 * D), D ** -0.5, 0.21875, ((0, 4),))
    w_out = gaussian(splits[4], (D, D), (D // 16) ** -0.5, 0.875, ((0, 4),))
    w_in = gaussian(splits[5], (D, 2 * FF), D ** -0.5, 0.21875, ((0, 4),))
    w_down = gaussian(splits[6], (FF, D), FF ** -0.5, 0.1875, ((0, 4),))
    gain_attn = jnp.clip(1.0 + 0.1 * jax.random.normal(splits[7], (D,), jnp.float32), 0.5, 1.5).astype(jnp.bfloat16)
    gain_mlp = jnp.clip(1.0 + 0.1 * jax.random.normal(splits[8], (D,), jnp.float32), 0.5, 1.5).astype(jnp.bfloat16)
    return {"inputs": inputs, "positions": positions, "cotangent": cotangent, "w_qkv": w_qkv, "w_out": w_out, "w_in": w_in, "w_down": w_down, "gain_attn": gain_attn, "gain_mlp": gain_mlp}


eps = 1e-05
rope_base = 10000.0
query_block = 512
masked_score = -1e+30

@jax.custom_vjp
def low(v):
    return lax.optimization_barrier(v.astype(jnp.bfloat16)).astype(jnp.float32)

@jax.custom_vjp
def low_back(v):
    return v

def low_keep(v):
    return (low(v), None)

def low_pass(kept, grad):
    return (grad,)

def back_keep(v):
    return (v, None)

def back_low(kept, grad):
    return (low(grad),)
low.defvjp(low_keep, low_pass)
low_back.defvjp(back_keep, back_low)

def layer_norm(values, gain):
    center = values - lax.optimization_barrier(jnp.mean(values, axis=-1, keepdims=True))
    spread = lax.optimization_barrier(jnp.mean(center * center, axis=-1, keepdims=True))
    return center * lax.rsqrt(spread + eps) * gain

def rotary(values, token_pos):
    half = values.shape[-1] // 2
    ladder = jnp.arange(half).astype(jnp.float32) * (2.0 / values.shape[-1])
    freqs = rope_base ** (-ladder)
    angles = token_pos.astype(jnp.float32)[:, None] * freqs[None, :]
    cosine = jnp.concatenate([jnp.cos(angles), jnp.cos(angles)], axis=-1)[:, None, :]
    sine = jnp.concatenate([jnp.sin(angles), jnp.sin(angles)], axis=-1)[:, None, :]
    turned = jnp.concatenate([-values[..., half:], values[..., :half]], axis=-1)
    return values * cosine + turned * sine

def attend(queries, keys, values, token_pos):
    length = queries.shape[0]
    width = query_block + 2 * HALF_WINDOW
    scale = HEAD_DIM ** (-0.5)
    keys_pad = jnp.pad(keys, ((HALF_WINDOW, HALF_WINDOW), (0, 0), (0, 0)))
    values_pad = jnp.pad(values, ((HALF_WINDOW, HALF_WINDOW), (0, 0), (0, 0)))
    pos_pad = jnp.pad(token_pos, (HALF_WINDOW, HALF_WINDOW))
    index_pad = jnp.pad(jnp.arange(length, dtype=jnp.int32), (HALF_WINDOW, HALF_WINDOW), constant_values=-1000000)

    def block(number):
        start = (number * query_block).astype(jnp.int32)
        query_rows = lax.dynamic_slice_in_dim(queries, start, query_block, 0)
        key_rows = lax.dynamic_slice_in_dim(keys_pad, start, width, 0)
        value_rows = lax.dynamic_slice_in_dim(values_pad, start, width, 0)
        query_pos = lax.dynamic_slice_in_dim(token_pos, start, query_block, 0)
        key_pos = lax.dynamic_slice_in_dim(pos_pad, start, width, 0)
        key_index = lax.dynamic_slice_in_dim(index_pad, start, width, 0)
        query_index = start + jnp.arange(query_block, dtype=jnp.int32)
        offset = key_index[None, :] - query_index[:, None]
        allowed = (jnp.abs(offset) <= HALF_WINDOW) & (query_pos[:, None] - key_pos[None, :] == -offset)
        scores = jnp.einsum('qhd,khd->hqk', query_rows, key_rows, precision=lax.Precision.HIGHEST) * scale
        scores = low_back(scores)
        scores = jnp.where(allowed[None], scores, masked_score)
        top = lax.optimization_barrier(jnp.max(scores, axis=-1, keepdims=True))
        weights = jnp.exp(scores - top)
        weights = low(weights / lax.optimization_barrier(jnp.sum(weights, axis=-1, keepdims=True)))
        return jnp.einsum('hqk,khd->qhd', weights, value_rows, precision=lax.Precision.HIGHEST)
    blocks = lax.map(jax.checkpoint(block), jnp.arange(length // query_block, dtype=jnp.int32))
    return blocks.reshape(length, HEADS, HEAD_DIM)

def stream_layer(tokens, token_pos, w_qkv, w_out, w_in, w_down, gain_attn, gain_mlp):
    length = tokens.shape[0]
    high = lax.Precision.HIGHEST
    normed = low(layer_norm(tokens, gain_attn))
    mixed = low_back(jnp.dot(normed, w_qkv, precision=high))
    queries = mixed[:, :D].reshape(length, HEADS, HEAD_DIM)
    keys = mixed[:, D:2 * D].reshape(length, HEADS, HEAD_DIM)
    values = mixed[:, 2 * D:].reshape(length, HEADS, HEAD_DIM)
    queries = low(rotary(queries, token_pos))
    keys = low(rotary(keys, token_pos))
    values = low(values)
    attended = low(low_back(attend(queries, keys, values, token_pos))).reshape(length, D)
    middle = tokens + low_back(jnp.dot(attended, w_out, precision=high))
    normed_mlp = low(layer_norm(middle, gain_mlp))
    gate_up = low_back(jnp.dot(normed_mlp, w_in, precision=high))
    hidden = low(jax.nn.gelu(gate_up[:, :FF], approximate=False) * gate_up[:, FF:])
    return middle + jnp.dot(hidden, w_down, precision=high)

def reference(inputs, positions, cotangent, w_qkv, w_out, w_in, w_down, gain_attn, gain_mlp):
    floats = tuple((item.astype(jnp.float32) for item in (inputs, w_qkv, w_out, w_in, w_down, gain_attn, gain_mlp)))

    def layer(tokens, wq, wo, wi, wd, ga, gm):

        def one_stream(carry, item):
            return (carry, jax.checkpoint(stream_layer)(item[0], item[1], wq, wo, wi, wd, ga, gm))
        unused, result = lax.scan(one_stream, None, (tokens, positions))
        return result
    result, pullback = jax.vjp(layer, *floats)
    grads = pullback(cotangent.astype(jnp.float32))
    return (result.astype(jnp.bfloat16), grads[0], grads[1], grads[2], grads[3], grads[4], grads[5], grads[6])
```

```python
import functools
import math

import jax
import jax.numpy as jnp
from jax import lax
from jax.experimental import pallas as pl
from jax.experimental.pallas import tpu as pltpu
from jax.sharding import PartitionSpec as P

D = 768
HEADS = 12
HEAD_DIM = 64
FF = 1152
HALF_WINDOW = 64


eps = 1e-05
rope_base = 10000.0
masked_score = -1e30


def with_halo(cells, sides, width):
    for axis, dim in sides:
        count = lax.axis_size(axis)
        ends = count - 1
        head = lax.slice_in_dim(cells, 0, width, axis=dim)
        tail = lax.slice_in_dim(cells, cells.shape[dim] - width, cells.shape[dim], axis=dim)
        cells = jnp.concatenate(
            [
                lax.ppermute(tail, axis, [(i, (i + 1) % count) for i in range(ends)]),
                cells,
                lax.ppermute(head, axis, [((i + 1) % count, i) for i in range(ends)]),
            ],
            axis=dim,
        )
    return cells


def layer_norm(values, gain):
    center = values - jnp.mean(values, axis=-1, keepdims=True)
    spread = jnp.mean(center * center, axis=-1, keepdims=True)
    return center * lax.rsqrt(spread + eps) * gain


def rotary(values, token_pos):
    half = values.shape[-1] // 2
    ladder = jnp.arange(half).astype(jnp.float32) * (2.0 / values.shape[-1])
    freqs = rope_base ** (-ladder)
    angles = token_pos.astype(jnp.float32)[:, None] * freqs[None, :]
    cosine = jnp.concatenate([jnp.cos(angles), jnp.cos(angles)], axis=-1)[:, None, :]
    sine = jnp.concatenate([jnp.sin(angles), jnp.sin(angles)], axis=-1)[:, None, :]
    turned = jnp.concatenate([-values[..., half:], values[..., :half]], axis=-1)
    return values * cosine + turned * sine


def window_mask(token_pos, wide_flags, count):
    offsets = jnp.arange(count + 2 * HALF_WINDOW, dtype=jnp.int32) - HALF_WINDOW
    offset = offsets[None, :] - jnp.arange(count, dtype=jnp.int32)[:, None]
    flag_float = wide_flags.astype(jnp.float32)[None, :]
    earlier = token_pos[:, None] >= -offset
    later = flag_float - 1.0 >= offset.astype(jnp.float32)
    return (
        (jnp.abs(offset) <= HALF_WINDOW)
        & (flag_float > 0.5)
        & jnp.where(offset < 0, earlier, later)
    )


def matmul_left(left, right):
    return lax.dot_general(
        left, right, (((0,), (0,)), ((), ())), preferred_element_type=jnp.float32
    )


def matmul_right(left, right):
    return lax.dot_general(
        left, right, (((1,), (1,)), ((), ())), preferred_element_type=jnp.float32
    )


def pack_rows(pieces, groups):
    joined = jnp.concatenate([piece.reshape(groups, -1) for piece in pieces], axis=1)
    return joined


def unpack_row(flat_row, pieces, groups):
    results = []
    offset = 0
    for piece in pieces:
        shape = (piece.shape[0] // groups,) + piece.shape[1:]
        size = math.prod(shape)
        results.append(flat_row[offset : offset + size].reshape(shape))
        offset = offset + size
    return results


MESH = pl.DeviceIdType.MESH
PAD = 32
SHARES = ((48, 1152), (48, 384), (48, 1152), (80, 384))
BIT1_FIRST = (True, True, False, False)


def partner(me, step):
    return me + step * (1 - 2 * ((me // step) % 2))


def place():
    me, z = lax.axis_index("seq"), lax.axis_index("fsdp")
    core, b1, b2 = me % 2, (me // 2) % 2, (me // 4) % 2
    return me, z, core, b1, b2


def greet(me, z):
    barrier = pltpu.get_barrier_semaphore()
    for step in (1, 2, 4):
        pl.semaphore_signal(
            barrier, inc=1, device_id={"seq": partner(me, step)}, device_id_type=MESH
        )
    for step in (1, 2, 3):
        pl.semaphore_signal(
            barrier, inc=1, device_id={"fsdp": (z + step) % 4}, device_id_type=MESH
        )
    pl.semaphore_wait(barrier, 6)


def rows(block, size, count=1):
    return pl.ds(pl.multiple_of(block * size, 16), size * count)


def cols(half, size):
    return pl.ds(pl.multiple_of(half * size, 128), size)


def push(src, dst, send, recv, target):
    return pltpu.make_async_remote_copy(
        src_ref=src, dst_ref=dst, send_sem=send, recv_sem=recv,
        device_id=target, device_id_type=MESH,
    )


def gather_kernel(*refs):
    ins, outs = refs[:4], refs[4:8]
    local, zs, zr, fs, s1, r1, s2, r2, s3, r3 = refs[8:]
    me, z, core, b1, b2 = place()
    quarter = b1 + 2 * b2
    greet(me, z)
    inner = (z == 1) | (z == 2)
    sent = []
    own = []
    for w, (r, c) in enumerate(SHARES):
        src = ins[w].at[rows(quarter, r), cols(core, c)]
        dst = outs[w].at[z, rows(quarter, r), cols(core, c)]
        up = push(src, dst, zs.at[w, 0], zr.at[w, z], {"fsdp": lax.rem(z + 1, 4)})
        down = push(src, dst, zs.at[w, 1], zr.at[w, z], {"fsdp": lax.rem(z + 3, 4)})
        own.append((up, down))
        pl.when(z < 3)(up.start)
        pl.when(z > 0)(down.start)
    copies = []
    for w in range(4):
        copy = pltpu.make_async_copy(ins[w], outs[w].at[z], local.at[w])
        copy.start()
        copies.append(copy)
    first = (z + 3) % 4 - 2 * ((3 - z) // 3)
    last = 3 * (1 - z // 2)
    second = 6 - z - first - last
    origins = (first, second, last)
    onward = ((z + 1) % 4, (z + 3) % 4, (3 * z + 1) % 4)
    events = [(k, w) for k in range(3) for w in range(4)]
    forwards, stage1, stage2, stage3 = {}, {}, {}, {}

    def arrive(k, w):
        r, c = SHARES[w]
        o = origins[k]
        mine = outs[w].at[o, rows(quarter, r), cols(core, c)]
        forward = push(mine, mine, fs.at[w, k], zr.at[w, o], {"fsdp": onward[k]})
        forwards[k, w] = forward
        forward.wait_recv()
        pl.when(inner)(forward.start)
        step = 2 if BIT1_FIRST[w] else 4
        copy = push(mine, mine, s1.at[w, k], r1.at[w, k], {"seq": partner(me, step)})
        copy.start()
        stage1[k, w] = copy

    def pair(k, w):
        r, c = SHARES[w]
        o = origins[k]
        stage1[k, w].wait_recv()
        half = cols(core, c)
        if BIT1_FIRST[w]:
            blocks = [outs[w].at[o, rows(2 * b2, r, 2), half]]
            step = 4
        else:
            blocks = [outs[w].at[o, rows(b1 + 2 * j, r), half] for j in range(2)]
            step = 2
        stage2[k, w] = []
        for j, block in enumerate(blocks):
            copy = push(block, block, s2.at[w, k, j], r2.at[w, k, j], {"seq": partner(me, step)})
            copy.start()
            stage2[k, w].append(copy)

    def across(k, w):
        r, c = SHARES[w]
        for copy in stage2[k, w]:
            copy.wait_recv()
        block = outs[w].at[origins[k], :, cols(core, c)]
        copy = push(block, block, s3.at[w, k], r3.at[w, k], {"seq": partner(me, 1)})
        copy.start()
        stage3[k, w] = copy

    for t in range(len(events) + 4):
        if t < len(events):
            arrive(*events[t])
        if 0 <= t - 2 < len(events):
            pair(*events[t - 2])
        if 0 <= t - 4 < len(events):
            across(*events[t - 4])
    for event in events:
        stage3[event].wait_recv()
    for copy in copies:
        copy.wait()
    for up, down in own:
        pl.when(z < 3)(up.wait_send)
        pl.when(z > 0)(down.wait_send)
    for event in events:
        pl.when(inner)(forwards[event].wait_send)
        stage1[event].wait_send()
        for copy in stage2[event]:
            copy.wait_send()
        stage3[event].wait_send()


def gather_weights(shards):
    sem = pltpu.SemaphoreType.DMA
    return pl.pallas_call(
        gather_kernel,
        out_shape=[jax.ShapeDtypeStruct((4, 4 * r, 2 * c), jnp.bfloat16) for r, c in SHARES],
        in_specs=[pl.BlockSpec(memory_space=pl.ANY)] * 4,
        out_specs=[pl.BlockSpec(memory_space=pl.ANY)] * 4,
        scratch_shapes=[
            sem((4,)), sem((4, 2)), sem((4, 4)), sem((4, 3)), sem((4, 3)), sem((4, 3)),
            sem((4, 3, 2)), sem((4, 3, 2)), sem((4, 3)), sem((4, 3)),
        ],
        compiler_params=pltpu.CompilerParams(collective_id=0, has_side_effects=True),
    )(*shards)


def reduce_kernel(*refs):
    ins, outs = refs[:4], refs[4:8]
    cb, cs, b1s, s1s, b2s, s2s, bz, ag = (refs[8 + 4 * i : 12 + 4 * i] for i in range(8))
    csem, sem1, sem2, zsem, asem = refs[40:]
    me, z, core, b1, b2 = place()
    quarter = b1 + 2 * b2
    greet(me, z)
    f32, low = jnp.float32, jnp.bfloat16
    sent = []
    table = {}

    def go(key, src, dst, sems, target):
        copy = push(src, dst, sems.at[0], sems.at[1], target)
        copy.start()
        sent.append(copy)
        table.setdefault(key, []).append(copy)

    def take(key):
        for copy in table[key]:
            copy.wait_recv()

    def begin(w):
        r, c = SHARES[w]
        src = ins[w].at[:, :, cols(1 - core, c)]
        go((0, w), src, cb[w], csem.at[w], {"seq": partner(me, 1)})

    def core_sum(w):
        r, c = SHARES[w]
        take((0, w))

        def body(i, carry):
            part = (i // 4, pl.ds(pl.multiple_of((i % 4) * r, 16), r))
            mine = ins[w][part[0], part[1], cols(core, c)].astype(f32)
            cs[w][part[0], part[1], :] = (mine + cb[w][part[0], part[1], :].astype(f32)).astype(low)
            return carry

        lax.fori_loop(0, 16, body, 0)
        if BIT1_FIRST[w]:
            src = cs[w].at[:, rows(2 * (1 - b2), r, 2), :]
            go((1, w), src, b1s[w], sem1.at[w, 0], {"seq": partner(me, 4)})
        else:
            for j in range(2):
                src = cs[w].at[:, rows(1 - b1 + 2 * j, r), :]
                dst = b1s[w].at[:, pl.ds(j * r, r), :]
                go((1, w), src, dst, sem1.at[w, j], {"seq": partner(me, 2)})

    def pair_sum(w):
        r, c = SHARES[w]
        take((1, w))

        def body(i, carry):
            o, j = i // 2, i % 2
            block = 2 * b2 + j if BIT1_FIRST[w] else b1 + 2 * j
            there = pl.ds(pl.multiple_of(j * r, 16), r)
            mine = cs[w][o, rows(block, r), :].astype(f32)
            s1s[w][o, there, :] = (mine + b1s[w][o, there, :].astype(f32)).astype(low)
            return carry

        lax.fori_loop(0, 8, body, 0)
        bit, step = (b1, 2) if BIT1_FIRST[w] else (b2, 4)
        src = s1s[w].at[:, rows(1 - bit, r), :]
        go((2, w), src, b2s[w], sem2.at[w], {"seq": partner(me, step)})

    def share_sum(w):
        r, c = SHARES[w]
        take((2, w))
        bit = b1 if BIT1_FIRST[w] else b2

        def body(o, carry):
            mine = s1s[w][o, rows(bit, r), :].astype(f32)
            s2s[w][o] = (mine + b2s[w][o].astype(f32)).astype(low)
            return carry

        lax.fori_loop(0, 4, body, 0)
        for d in (2, 1, 3):
            to = (z + d) % 4
            go((3, w), s2s[w].at[to], bz[w].at[d - 1], zsem.at[w, d - 1], {"fsdp": to})

    def owner_sum(w):
        r, c = SHARES[w]
        take((3, w))
        total = s2s[w][z].astype(f32)
        for d in range(3):
            total = total + bz[w][d].astype(f32)
        ag[w][rows(quarter, r), cols(core, c)] = total.astype(low)
        block = ag[w].at[rows(quarter, r), cols(core, c)]
        step = 2 if BIT1_FIRST[w] else 4
        go((4, w), block, block, asem.at[w, 0], {"seq": partner(me, step)})

    def spread(w):
        r, c = SHARES[w]
        take((4, w))
        half = cols(core, c)
        if BIT1_FIRST[w]:
            block = ag[w].at[rows(2 * b2, r, 2), half]
            go((5, w), block, block, asem.at[w, 1], {"seq": partner(me, 4)})
        else:
            for j in range(2):
                block = ag[w].at[rows(b1 + 2 * j, r), half]
                go((5, w), block, block, asem.at[w, 1 + j], {"seq": partner(me, 2)})

    def across(w):
        r, c = SHARES[w]
        take((5, w))
        block = ag[w].at[:, cols(core, c)]
        go((6, w), block, block, asem.at[w, 3], {"seq": partner(me, 1)})

    def finish(w):
        r, c = SHARES[w]
        take((6, w))

        def body(i, carry):
            part = pl.ds(pl.multiple_of(i * r, 16), r)
            outs[w][part, :] = ag[w][part, :].astype(f32)
            return carry

        lax.fori_loop(0, 4, body, 0)

    order = (2, 0, 3, 1)
    steps = (core_sum, pair_sum, share_sum, owner_sum, spread, across, finish)
    for w in order:
        begin(w)
    for t in range(len(steps) + 3):
        for i, w in enumerate(order):
            if 0 <= t - i < len(steps):
                steps[t - i](w)
    for copy in sent:
        copy.wait_send()


def reduce_grads(parts):
    sem = pltpu.SemaphoreType.DMA
    vmem = lambda shape: pltpu.VMEM(shape, jnp.bfloat16)
    half = [vmem((4, 4 * r, c)) for r, c in SHARES]
    two = [vmem((4, 2 * r, c)) for r, c in SHARES]
    one = [vmem((4, r, c)) for r, c in SHARES]
    slots = [vmem((3, r, c)) for r, c in SHARES]
    whole = [vmem((4 * r, 2 * c)) for r, c in SHARES]
    return pl.pallas_call(
        reduce_kernel,
        out_shape=[jax.ShapeDtypeStruct((4 * r, 2 * c), jnp.float32) for r, c in SHARES],
        in_specs=[pl.BlockSpec(memory_space=pltpu.VMEM)] * 4,
        out_specs=[pl.BlockSpec(memory_space=pltpu.VMEM)] * 4,
        scratch_shapes=half + half + two + two + one + one + slots + whole
        + [sem((4, 2)), sem((4, 2, 2)), sem((4, 2)), sem((4, 3, 2)), sem((4, 4, 2))],
        compiler_params=pltpu.CompilerParams(
            collective_id=1, has_side_effects=True, vmem_limit_bytes=56 * 1024 * 1024
        ),
    )(*parts)


def on_device(inputs, positions, cotangent, w_qkv, w_out, w_in, w_down, gain_attn, gain_mlp):
    gains = jnp.concatenate([gain_attn, gain_mlp])
    gains = jnp.pad(gains[None], ((0, PAD - 1), (0, D - gains.shape[0])))
    packed = jnp.concatenate([w_down, gains], axis=0)
    full_qkv, full_out, full_in, full_packed = gather_weights([w_qkv, w_out, w_in, packed])
    full_qkv = full_qkv.reshape(D, 3 * D)
    full_out = full_out.reshape(D, D)
    full_in = full_in.reshape(D, 2 * FF)
    owned_rows = w_down.shape[0]
    full_down = full_packed[:, :owned_rows].reshape(FF, D)
    held = gain_attn.shape[0]
    gain_first = full_packed[:, owned_rows, :held].reshape(D).astype(jnp.float32)
    gain_second = full_packed[:, owned_rows, held : 2 * held].reshape(D).astype(jnp.float32)
    scale = HEAD_DIM ** (-0.5)
    tokens = inputs[0].astype(jnp.float32)
    token_pos = positions[0]
    count = tokens.shape[0]
    extent = count + 2 * HALF_WINDOW
    normed, norm_back = jax.vjp(layer_norm, tokens, gain_first)
    normed_low = normed.astype(jnp.bfloat16)
    mixed = jnp.dot(normed_low, full_qkv, preferred_element_type=jnp.float32)
    query_raw = mixed[:, :D].reshape(count, HEADS, HEAD_DIM)
    key_raw = mixed[:, D : 2 * D].reshape(count, HEADS, HEAD_DIM)
    value_low = mixed[:, 2 * D :].astype(jnp.bfloat16)
    query_rot, query_back = jax.vjp(lambda piece: rotary(piece, token_pos), query_raw)
    key_rot, key_back = jax.vjp(lambda piece: rotary(piece, token_pos), key_raw)
    query_low = query_rot.astype(jnp.bfloat16)
    flags = (jnp.minimum(token_pos, 127) + 1).astype(jnp.bfloat16)
    key_value = jnp.concatenate(
        [key_rot.reshape(count, D).astype(jnp.bfloat16), value_low, flags[:, None]], axis=1
    )
    wide_kv = with_halo(key_value, (("seq", 0),), HALF_WINDOW)
    wide_flags = wide_kv[:, 2 * D]
    keys_wide = wide_kv[:, :D].reshape(extent, HEADS, HEAD_DIM)
    values_wide = wide_kv[:, D : 2 * D].reshape(extent, HEADS, HEAD_DIM)
    allowed = window_mask(token_pos, wide_flags, count)

    def score_table():
        raw = (
            jnp.einsum("qhd,khd->hqk", query_low, keys_wide, preferred_element_type=jnp.float32)
            * scale
        )
        return jnp.where(allowed[None], raw, masked_score)

    scores = score_table()
    top = jnp.max(scores, axis=-1, keepdims=True)
    expo = jnp.exp(scores - top)
    totals = jnp.sum(expo, axis=-1, keepdims=True)
    logsum = top + jnp.log(totals)
    probs_low = (expo / totals).astype(jnp.bfloat16)
    attended = jnp.einsum(
        "hqk,khd->qhd", probs_low, values_wide, preferred_element_type=jnp.float32
    )
    attended_low = attended.reshape(count, D).astype(jnp.bfloat16)
    middle = tokens + jnp.dot(attended_low, full_out, preferred_element_type=jnp.float32)
    normed_mlp, mlp_norm_back = jax.vjp(layer_norm, middle, gain_second)
    normed_mlp_low = normed_mlp.astype(jnp.bfloat16)
    gate_up = jnp.dot(normed_mlp_low, full_in, preferred_element_type=jnp.float32)

    def geglu(paired):
        return jax.nn.gelu(paired[:, :FF], approximate=False) * paired[:, FF:]

    hidden, geglu_back = jax.vjp(geglu, gate_up)
    hidden_low = hidden.astype(jnp.bfloat16)
    result = middle + jnp.dot(hidden_low, full_down, preferred_element_type=jnp.float32)
    grad_result = cotangent[0]
    grad_down_local = matmul_left(hidden_low, grad_result)
    grad_hidden = matmul_right(grad_result, full_down)
    grad_gate_up = geglu_back(grad_hidden)[0].astype(jnp.bfloat16)
    grad_in_local = matmul_left(normed_mlp_low, grad_gate_up)
    grad_normed_mlp = matmul_right(grad_gate_up, full_in)
    grad_middle_norm, grad_gain_second = mlp_norm_back(grad_normed_mlp)
    grad_middle = grad_result.astype(jnp.float32) + grad_middle_norm
    grad_branch = grad_middle.astype(jnp.bfloat16)
    grad_out_local = matmul_left(attended_low, grad_branch)
    grad_attended = (
        matmul_right(grad_branch, full_out).reshape(count, HEADS, HEAD_DIM).astype(jnp.bfloat16)
    )
    probs = jnp.exp(score_table() - logsum)
    probs_low = probs.astype(jnp.bfloat16)
    grad_probs = jnp.einsum(
        "qhd,khd->hqk", grad_attended, values_wide, preferred_element_type=jnp.float32
    )
    row_dot = jnp.sum(probs * grad_probs, axis=-1, keepdims=True)
    grad_scores = (probs * (grad_probs - row_dot)).astype(jnp.bfloat16)
    grad_query = (
        jnp.einsum("hqk,khd->qhd", grad_scores, keys_wide, preferred_element_type=jnp.float32)
        * scale
    )
    grad_keys_wide = (
        jnp.einsum("hqk,qhd->khd", grad_scores, query_low, preferred_element_type=jnp.float32)
        * scale
    )
    grad_values_wide = jnp.einsum(
        "hqk,qhd->khd", probs_low, grad_attended, preferred_element_type=jnp.float32
    )
    grad_wide = jnp.concatenate(
        [grad_keys_wide.reshape(extent, D), grad_values_wide.reshape(extent, D)], axis=1
    )
    lanes = lax.axis_size("seq")
    above = lax.ppermute(
        grad_wide[extent - HALF_WINDOW :].astype(jnp.bfloat16),
        "seq",
        [(i, i + 1) for i in range(lanes - 1)],
    )
    below = lax.ppermute(
        grad_wide[:HALF_WINDOW].astype(jnp.bfloat16),
        "seq",
        [(i + 1, i) for i in range(lanes - 1)],
    )
    returned = jnp.concatenate([above, below], axis=0).astype(jnp.float32)
    grad_own = grad_wide[HALF_WINDOW : HALF_WINDOW + count] + returned
    grad_key = key_back(grad_own[:, :D].reshape(count, HEADS, HEAD_DIM))[0]
    grad_q = query_back(grad_query)[0]
    grad_mixed = jnp.concatenate(
        [grad_q.reshape(count, D), grad_key.reshape(count, D), grad_own[:, D:]], axis=1
    ).astype(jnp.bfloat16)
    grad_qkv_local = matmul_left(normed_low, grad_mixed)
    grad_normed = matmul_right(grad_mixed, full_qkv)
    grad_tokens_norm, grad_gain_first = norm_back(grad_normed)
    grad_tokens = grad_middle + grad_tokens_norm
    if lanes == 8:
        gain_rows = jnp.concatenate(
            [grad_gain_first.reshape(4, 1, held), grad_gain_second.reshape(4, 1, held)], axis=2
        )
        gain_rows = jnp.pad(gain_rows, ((0, 0), (0, PAD - 1), (0, D - 2 * held)))
        grad_packed = jnp.concatenate(
            [grad_down_local.reshape(4, owned_rows, D), gain_rows], axis=1
        )
        parts = (
            grad_qkv_local.reshape(4, held, 3 * D),
            grad_out_local.reshape(4, held, D),
            grad_in_local.reshape(4, held, 2 * FF),
            grad_packed,
        )
        grad_qkv, grad_out, grad_in, packed = reduce_grads(
            [part.astype(jnp.bfloat16) for part in parts]
        )
        return (
            result[None].astype(jnp.bfloat16),
            grad_tokens[None],
            grad_qkv,
            grad_out,
            grad_in,
            packed[:owned_rows],
            packed[owned_rows, :held],
            packed[owned_rows, held : 2 * held],
        )
    owned = (
        lax.psum_scatter(
            grad_qkv_local.astype(jnp.bfloat16), "fsdp", scatter_dimension=0, tiled=True
        ).astype(jnp.float32),
        lax.psum_scatter(
            grad_out_local.astype(jnp.bfloat16), "fsdp", scatter_dimension=0, tiled=True
        ).astype(jnp.float32),
        lax.psum_scatter(
            grad_in_local.astype(jnp.bfloat16), "fsdp", scatter_dimension=0, tiled=True
        ).astype(jnp.float32),
        lax.psum_scatter(
            grad_down_local.astype(jnp.bfloat16), "fsdp", scatter_dimension=0, tiled=True
        ).astype(jnp.float32),
        lax.psum_scatter(
            grad_gain_first.astype(jnp.bfloat16), "fsdp", scatter_dimension=0, tiled=True
        ).astype(jnp.float32),
        lax.psum_scatter(
            grad_gain_second.astype(jnp.bfloat16), "fsdp", scatter_dimension=0, tiled=True
        ).astype(jnp.float32),
    )
    owned_flat = pack_rows(owned, 1)
    owned_share = owned_flat.shape[1] // lanes
    lane_part = lax.psum_scatter(
        owned_flat.reshape(lanes, owned_share), "seq", scatter_dimension=0, tiled=True
    )
    summed_row = (
        lax.all_gather(lane_part.astype(jnp.bfloat16), "seq", axis=0, tiled=True)
        .astype(lane_part.dtype)
        .reshape(-1)
    )
    grad_qkv, grad_out, grad_in, grad_down, grad_gain_attn, grad_gain_mlp = unpack_row(
        summed_row, owned, 1
    )
    return (
        result[None].astype(jnp.bfloat16),
        grad_tokens[None],
        grad_qkv,
        grad_out,
        grad_in,
        grad_down,
        grad_gain_attn,
        grad_gain_mlp,
    )


def solution(mesh):
    in_specs = (
        P("fsdp", "seq", None),
        P("fsdp", "seq"),
        P("fsdp", "seq", None),
        P("fsdp", None),
        P("fsdp", None),
        P("fsdp", None),
        P("fsdp", None),
        P("fsdp"),
        P("fsdp"),
    )
    out_specs = (
        P("fsdp", "seq", None),
        P("fsdp", "seq", None),
        P("fsdp", None),
        P("fsdp", None),
        P("fsdp", None),
        P("fsdp", None),
        P("fsdp"),
        P("fsdp"),
    )
    return jax.shard_map(
        on_device, mesh=mesh, in_specs=in_specs, out_specs=out_specs, check_vma=False
    )
```

```python
import functools
import math

import jax
import jax.numpy as jnp
from jax import lax
from jax.experimental import pallas as pl
from jax.experimental.pallas import tpu as pltpu
from jax.sharding import PartitionSpec as P

D = 768
HEADS = 12
HEAD_DIM = 64
FF = 1152
HALF_WINDOW = 64


eps = 1e-05
rope_base = 10000.0
masked_score = -1e30


def with_halo(cells, sides, width):
    for axis, dim in sides:
        count = lax.axis_size(axis)
        ends = count - 1
        head = lax.slice_in_dim(cells, 0, width, axis=dim)
        tail = lax.slice_in_dim(cells, cells.shape[dim] - width, cells.shape[dim], axis=dim)
        cells = jnp.concatenate(
            [
                lax.ppermute(tail, axis, [(i, (i + 1) % count) for i in range(ends)]),
                cells,
                lax.ppermute(head, axis, [((i + 1) % count, i) for i in range(ends)]),
            ],
            axis=dim,
        )
    return cells


def layer_norm(values, gain):
    center = values - jnp.mean(values, axis=-1, keepdims=True)
    spread = jnp.mean(center * center, axis=-1, keepdims=True)
    return center * lax.rsqrt(spread + eps) * gain


def rotary(values, token_pos):
    half = values.shape[-1] // 2
    ladder = jnp.arange(half).astype(jnp.float32) * (2.0 / values.shape[-1])
    freqs = rope_base ** (-ladder)
    angles = token_pos.astype(jnp.float32)[:, None] * freqs[None, :]
    cosine = jnp.concatenate([jnp.cos(angles), jnp.cos(angles)], axis=-1)[:, None, :]
    sine = jnp.concatenate([jnp.sin(angles), jnp.sin(angles)], axis=-1)[:, None, :]
    turned = jnp.concatenate([-values[..., half:], values[..., :half]], axis=-1)
    return values * cosine + turned * sine


def window_mask(token_pos, wide_flags, count):
    offsets = jnp.arange(count + 2 * HALF_WINDOW, dtype=jnp.int32) - HALF_WINDOW
    offset = offsets[None, :] - jnp.arange(count, dtype=jnp.int32)[:, None]
    flag_float = wide_flags.astype(jnp.float32)[None, :]
    earlier = token_pos[:, None] >= -offset
    later = flag_float - 1.0 >= offset.astype(jnp.float32)
    return (
        (jnp.abs(offset) <= HALF_WINDOW)
        & (flag_float > 0.5)
        & jnp.where(offset < 0, earlier, later)
    )


def matmul_left(left, right):
    return lax.dot_general(
        left, right, (((0,), (0,)), ((), ())), preferred_element_type=jnp.float32
    )


def matmul_right(left, right):
    return lax.dot_general(
        left, right, (((1,), (1,)), ((), ())), preferred_element_type=jnp.float32
    )


def pack_rows(pieces, groups):
    joined = jnp.concatenate([piece.reshape(groups, -1) for piece in pieces], axis=1)
    return joined


def unpack_row(flat_row, pieces, groups):
    results = []
    offset = 0
    for piece in pieces:
        shape = (piece.shape[0] // groups,) + piece.shape[1:]
        size = math.prod(shape)
        results.append(flat_row[offset : offset + size].reshape(shape))
        offset = offset + size
    return results


MESH = pl.DeviceIdType.MESH
PAD = 32
SHARES = ((48, 1152), (48, 384), (48, 1152), (80, 384))
BIT1_FIRST = (True, True, False, False)


def partner(me, step):
    return me + step * (1 - 2 * ((me // step) % 2))


def place():
    me, z = lax.axis_index("seq"), lax.axis_index("fsdp")
    core, b1, b2 = me % 2, (me // 2) % 2, (me // 4) % 2
    return me, z, core, b1, b2


def greet(me, z):
    barrier = pltpu.get_barrier_semaphore()
    for step in (1, 2, 4):
        pl.semaphore_signal(
            barrier, inc=1, device_id={"seq": partner(me, step)}, device_id_type=MESH
        )
    for step in (1, 2, 3):
        pl.semaphore_signal(
            barrier, inc=1, device_id={"fsdp": (z + step) % 4}, device_id_type=MESH
        )
    pl.semaphore_wait(barrier, 6)


def rows(block, size, count=1):
    return pl.ds(pl.multiple_of(block * size, 16), size * count)


def cols(half, size):
    return pl.ds(pl.multiple_of(half * size, 128), size)


def push(src, dst, send, recv, target):
    return pltpu.make_async_remote_copy(
        src_ref=src, dst_ref=dst, send_sem=send, recv_sem=recv,
        device_id=target, device_id_type=MESH,
    )


def gather_order():
    order = []
    for k in range(4):
        if k < 3:
            order += [(0, k, w) for w in range(4)]
        if k > 0:
            order += [(2, k - 1, w) for w in range(4)]
        if k < 3:
            order += [(1, k, w) for w in range(4)]
    return order


def gather_kernel(*refs):
    ins, outs = refs[:4], refs[4:8]
    local, zs, zr, fs, s1, r1, s2, r2, s3, r3 = refs[8:]
    me, z, core, b1, b2 = place()
    quarter = b1 + 2 * b2
    greet(me, z)
    inner = (z == 1) | (z == 2)
    sent = []
    own = []
    for w, (r, c) in enumerate(SHARES):
        src = ins[w].at[rows(quarter, r), cols(core, c)]
        dst = outs[w].at[z, rows(quarter, r), cols(core, c)]
        up = push(src, dst, zs.at[w, 0], zr.at[w, z], {"fsdp": lax.rem(z + 1, 4)})
        down = push(src, dst, zs.at[w, 1], zr.at[w, z], {"fsdp": lax.rem(z + 3, 4)})
        own.append((up, down))
        pl.when(z < 3)(up.start)
        pl.when(z > 0)(down.start)
    copies = []
    for w in range(4):
        copy = pltpu.make_async_copy(ins[w], outs[w].at[z], local.at[w])
        copy.start()
        copies.append(copy)
    first = (z + 3) % 4 - 2 * ((3 - z) // 3)
    last = 3 * (1 - z // 2)
    second = 6 - z - first - last
    origins = (first, second, last)
    onward = ((z + 1) % 4, (z + 3) % 4, (3 * z + 1) % 4)
    events = [(k, w) for k in range(3) for w in range(4)]
    forwards, stage1, stage2, stage3 = {}, {}, {}, {}

    def arrive(k, w):
        r, c = SHARES[w]
        o = origins[k]
        mine = outs[w].at[o, rows(quarter, r), cols(core, c)]
        forward = push(mine, mine, fs.at[w, k], zr.at[w, o], {"fsdp": onward[k]})
        forwards[k, w] = forward
        forward.wait_recv()
        pl.when(inner)(forward.start)
        step = 2 if BIT1_FIRST[w] else 4
        copy = push(mine, mine, s1.at[w, k], r1.at[w, k], {"seq": partner(me, step)})
        copy.start()
        stage1[k, w] = copy

    def pair(k, w):
        r, c = SHARES[w]
        o = origins[k]
        stage1[k, w].wait_recv()
        half = cols(core, c)
        if BIT1_FIRST[w]:
            blocks = [outs[w].at[o, rows(2 * b2, r, 2), half]]
            step = 4
        else:
            blocks = [outs[w].at[o, rows(b1 + 2 * j, r), half] for j in range(2)]
            step = 2
        stage2[k, w] = []
        for j, block in enumerate(blocks):
            copy = push(block, block, s2.at[w, k, j], r2.at[w, k, j], {"seq": partner(me, step)})
            copy.start()
            stage2[k, w].append(copy)

    def across(k, w):
        r, c = SHARES[w]
        for copy in stage2[k, w]:
            copy.wait_recv()
        block = outs[w].at[origins[k], :, cols(core, c)]
        copy = push(block, block, s3.at[w, k], r3.at[w, k], {"seq": partner(me, 1)})
        copy.start()
        stage3[k, w] = copy

    acts = (arrive, pair, across)
    for act, k, w in gather_order():
        acts[act](k, w)
    for event in events:
        stage3[event].wait_recv()
    for copy in copies:
        copy.wait()
    for up, down in own:
        pl.when(z < 3)(up.wait_send)
        pl.when(z > 0)(down.wait_send)
    for event in events:
        pl.when(inner)(forwards[event].wait_send)
        stage1[event].wait_send()
        for copy in stage2[event]:
            copy.wait_send()
        stage3[event].wait_send()


def gather_weights(shards):
    sem = pltpu.SemaphoreType.DMA
    return pl.pallas_call(
        gather_kernel,
        out_shape=[jax.ShapeDtypeStruct((4, 4 * r, 2 * c), jnp.bfloat16) for r, c in SHARES],
        in_specs=[pl.BlockSpec(memory_space=pltpu.VMEM)] * 4,
        out_specs=[pl.BlockSpec(memory_space=pl.ANY)] * 4,
        scratch_shapes=[
            sem((4,)), sem((4, 2)), sem((4, 4)), sem((4, 3)), sem((4, 3)), sem((4, 3)),
            sem((4, 3, 2)), sem((4, 3, 2)), sem((4, 3)), sem((4, 3)),
        ],
        compiler_params=pltpu.CompilerParams(
            collective_id=0, has_side_effects=True, vmem_limit_bytes=32 * 1024 * 1024
        ),
    )(*shards)


WIDE = 384
CHUNKS = ((2, 0), (0, 0), (2, 384), (0, 384), (2, 768), (0, 768), (3, 0), (1, 0))


def reduce_order():
    ahead = 4
    order = [("first", p) for p in range(ahead)]
    for t in range(4 + 6):
        for act, lag in (
            ("finish", 6), ("across", 5), ("spread", 4), ("owner", 3), ("share", 2), ("pair", 0)
        ):
            if 0 <= t - lag < 4:
                order.append((act, t - lag))
        if t + ahead < 4:
            order.append(("first", t + ahead))
    return order


def reduce_kernel(*refs):
    xin, yin, gin, outs = refs[:4], refs[4:8], refs[8], refs[9:13]
    xb, yb, gb = refs[13:17], refs[17:21], refs[21]
    cs, b1s, s1s, b2s, s2s, bz, ag = (refs[22 + 8 * i : 30 + 8 * i] for i in range(7))
    csem, sem1, sem2, zsem, asem = refs[78:]
    me, z, core, b1, b2 = place()
    quarter = b1 + 2 * b2
    greet(me, z)
    f32, low = jnp.float32, jnp.bfloat16
    sent = []
    table = {}

    def go(key, src, dst, sems, target):
        copy = push(src, dst, sems.at[0], sems.at[1], target)
        copy.start()
        sent.append(copy)
        table.setdefault(key, []).append(copy)

    def take(key):
        for copy in table[key]:
            copy.wait_recv()

    twin = {"seq": partner(me, 1)}
    lanes = cols(core, 128)
    for w in (2, 0, 3, 1):
        c = SHARES[w][1]
        go(("x", w), xin[w], xb[w].at[:, lanes], csem.at[0, w], twin)
        go(("x", w), yin[w].at[:, cols(1 - core, c)], yb[w].at[rows(core, 128)], csem.at[1, w], twin)
    go("g", gin.at[:, :, cols(1 - core, WIDE)], gb, csem.at[2, 0], twin)
    for w in (2, 0, 3, 1):
        xb[w][:, lanes] = xin[w][...]
        yb[w][rows(core, 128), :] = yin[w][:, cols(core, SHARES[w][1])]

    def product(i):
        w, start = CHUNKS[i]
        height = 4 * SHARES[w][0]
        if start == 0:
            take(("x", w))

        def body(o, carry):
            left = xb[w][pl.ds(pl.multiple_of(o * height, 16), height), :]
            right = yb[w][:, start : start + WIDE]
            cs[i][o] = jnp.dot(left, right, preferred_element_type=f32).astype(low)
            return carry

        lax.fori_loop(0, 4, body, 0)
        if w == 3:
            take("g")
            mine = gin[:, :, cols(core, WIDE)].astype(f32)
            cs[i][:, height - PAD :, :] = (mine + gb[...].astype(f32)).astype(low)

    def first(i):
        product(i)
        w = CHUNKS[i][0]
        r = SHARES[w][0]
        if BIT1_FIRST[w]:
            src = cs[i].at[:, rows(2 * (1 - b2), r, 2), :]
            go((1, i), src, b1s[i], sem1.at[i, 0], {"seq": partner(me, 4)})
        else:
            for j in range(2):
                src = cs[i].at[:, rows(1 - b1 + 2 * j, r), :]
                dst = b1s[i].at[:, pl.ds(j * r, r), :]
                go((1, i), src, dst, sem1.at[i, j], {"seq": partner(me, 2)})

    def pair(i):
        w = CHUNKS[i][0]
        r = SHARES[w][0]
        take((1, i))

        def body(t, carry):
            o, j = t // 2, t % 2
            block = 2 * b2 + j if BIT1_FIRST[w] else b1 + 2 * j
            there = pl.ds(pl.multiple_of(j * r, 16), r)
            mine = cs[i][o, rows(block, r), :].astype(f32)
            s1s[i][o, there, :] = (mine + b1s[i][o, there, :].astype(f32)).astype(low)
            return carry

        lax.fori_loop(0, 8, body, 0)
        bit, step = (b1, 2) if BIT1_FIRST[w] else (b2, 4)
        src = s1s[i].at[:, rows(1 - bit, r), :]
        go((2, i), src, b2s[i], sem2.at[i], {"seq": partner(me, step)})

    def share(i):
        w = CHUNKS[i][0]
        r = SHARES[w][0]
        take((2, i))
        bit = b1 if BIT1_FIRST[w] else b2

        def body(o, carry):
            mine = s1s[i][o, rows(bit, r), :].astype(f32)
            s2s[i][o] = (mine + b2s[i][o].astype(f32)).astype(low)
            return carry

        lax.fori_loop(0, 4, body, 0)
        for d in (2, 1, 3):
            to = (z + d) % 4
            go((3, i), s2s[i].at[to], bz[i].at[d - 1], zsem.at[i, d - 1], {"fsdp": to})

    def owner(i):
        w = CHUNKS[i][0]
        r = SHARES[w][0]
        take((3, i))
        total = s2s[i][z].astype(f32)
        for d in range(3):
            total = total + bz[i][d].astype(f32)
        ag[i][core, rows(quarter, r), :] = total.astype(low)
        block = ag[i].at[core, rows(quarter, r), :]
        step = 2 if BIT1_FIRST[w] else 4
        go((4, i), block, block, asem.at[i, 0], {"seq": partner(me, step)})

    def spread(i):
        w = CHUNKS[i][0]
        r = SHARES[w][0]
        take((4, i))
        if BIT1_FIRST[w]:
            block = ag[i].at[core, rows(2 * b2, r, 2), :]
            go((5, i), block, block, asem.at[i, 1], {"seq": partner(me, 4)})
        else:
            for j in range(2):
                block = ag[i].at[core, rows(b1 + 2 * j, r), :]
                go((5, i), block, block, asem.at[i, 1 + j], {"seq": partner(me, 2)})

    def across(i):
        take((5, i))
        block = ag[i].at[core]
        go((6, i), block, block, asem.at[i, 3], twin)

    def finish(i):
        w, start = CHUNKS[i]
        r, c = SHARES[w]
        take((6, i))

        def body(t, carry):
            part = pl.ds(pl.multiple_of(t * r, 16), r)
            for half in range(2):
                at = half * c + start
                outs[w][part, at : at + WIDE] = ag[i][half, part, :].astype(f32)
            return carry

        lax.fori_loop(0, 4, body, 0)

    acts = {
        "first": first, "pair": pair, "share": share, "owner": owner,
        "spread": spread, "across": across, "finish": finish,
    }
    for act, p in reduce_order():
        for i in (2 * p, 2 * p + 1):
            acts[act](i)
    for copy in sent:
        copy.wait_send()


def reduce_grads(lefts, rights, gain_rows):
    sem = pltpu.SemaphoreType.DMA
    vmem = lambda *shape: pltpu.VMEM(shape, jnp.bfloat16)
    heights = [SHARES[w][0] for w, start in CHUNKS]
    count = len(CHUNKS)
    return pl.pallas_call(
        reduce_kernel,
        out_shape=[jax.ShapeDtypeStruct((4 * r, 2 * c), jnp.float32) for r, c in SHARES],
        in_specs=[pl.BlockSpec(memory_space=pltpu.VMEM)] * 9,
        out_specs=[pl.BlockSpec(memory_space=pltpu.VMEM)] * 4,
        scratch_shapes=[vmem(16 * r, 256) for r, c in SHARES]
        + [vmem(256, c) for r, c in SHARES]
        + [vmem(4, PAD, WIDE)]
        + [vmem(4, 4 * r, WIDE) for r in heights]
        + [vmem(4, 2 * r, WIDE) for r in heights] * 2
        + [vmem(4, r, WIDE) for r in heights] * 2
        + [vmem(3, r, WIDE) for r in heights]
        + [vmem(2, 4 * r, WIDE) for r in heights]
        + [
            sem((3, 4, 2)), sem((count, 2, 2)), sem((count, 2)), sem((count, 3, 2)),
            sem((count, 4, 2)),
        ],
        compiler_params=pltpu.CompilerParams(
            collective_id=1, has_side_effects=True, vmem_limit_bytes=56 * 1024 * 1024
        ),
    )(*lefts, *rights, gain_rows)


def on_device(inputs, positions, cotangent, w_qkv, w_out, w_in, w_down, gain_attn, gain_mlp):
    gains = jnp.concatenate([gain_attn, gain_mlp])
    gains = jnp.pad(gains[None], ((0, PAD - 1), (0, D - gains.shape[0])))
    packed = jnp.concatenate([w_down, gains], axis=0)
    full_qkv, full_out, full_in, full_packed = gather_weights([w_qkv, w_out, w_in, packed])
    full_qkv = full_qkv.reshape(D, 3 * D)
    full_out = full_out.reshape(D, D)
    full_in = full_in.reshape(D, 2 * FF)
    owned_rows = w_down.shape[0]
    full_down = full_packed[:, :owned_rows].reshape(FF, D)
    held = gain_attn.shape[0]
    gain_first = full_packed[:, owned_rows, :held].reshape(D).astype(jnp.float32)
    gain_second = full_packed[:, owned_rows, held : 2 * held].reshape(D).astype(jnp.float32)
    scale = HEAD_DIM ** (-0.5)
    tokens = inputs[0].astype(jnp.float32)
    token_pos = positions[0]
    count = tokens.shape[0]
    extent = count + 2 * HALF_WINDOW
    normed, norm_back = jax.vjp(layer_norm, tokens, gain_first)
    normed_low = normed.astype(jnp.bfloat16)
    mixed = jnp.dot(normed_low, full_qkv, preferred_element_type=jnp.float32)
    query_raw = mixed[:, :D].reshape(count, HEADS, HEAD_DIM)
    key_raw = mixed[:, D : 2 * D].reshape(count, HEADS, HEAD_DIM)
    value_low = mixed[:, 2 * D :].astype(jnp.bfloat16)
    query_rot, query_back = jax.vjp(lambda piece: rotary(piece, token_pos), query_raw)
    key_rot, key_back = jax.vjp(lambda piece: rotary(piece, token_pos), key_raw)
    query_low = query_rot.astype(jnp.bfloat16)
    flags = (jnp.minimum(token_pos, 127) + 1).astype(jnp.bfloat16)
    key_value = jnp.concatenate(
        [key_rot.reshape(count, D).astype(jnp.bfloat16), value_low, flags[:, None]], axis=1
    )
    wide_kv = with_halo(key_value, (("seq", 0),), HALF_WINDOW)
    wide_flags = wide_kv[:, 2 * D]
    keys_wide = wide_kv[:, :D].reshape(extent, HEADS, HEAD_DIM)
    values_wide = wide_kv[:, D : 2 * D].reshape(extent, HEADS, HEAD_DIM)
    allowed = window_mask(token_pos, wide_flags, count)

    def score_table():
        raw = (
            jnp.einsum("qhd,khd->hqk", query_low, keys_wide, preferred_element_type=jnp.float32)
            * scale
        )
        return jnp.where(allowed[None], raw, masked_score)

    scores = score_table()
    top = jnp.max(scores, axis=-1, keepdims=True)
    expo = jnp.exp(scores - top)
    totals = jnp.sum(expo, axis=-1, keepdims=True)
    logsum = top + jnp.log(totals)
    probs_low = (expo / totals).astype(jnp.bfloat16)
    attended = jnp.einsum(
        "hqk,khd->qhd", probs_low, values_wide, preferred_element_type=jnp.float32
    )
    attended_low = attended.reshape(count, D).astype(jnp.bfloat16)
    middle = tokens + jnp.dot(attended_low, full_out, preferred_element_type=jnp.float32)
    normed_mlp, mlp_norm_back = jax.vjp(layer_norm, middle, gain_second)
    normed_mlp_low = normed_mlp.astype(jnp.bfloat16)
    gate_up = jnp.dot(normed_mlp_low, full_in, preferred_element_type=jnp.float32)

    def geglu(paired):
        return jax.nn.gelu(paired[:, :FF], approximate=False) * paired[:, FF:]

    hidden, geglu_back = jax.vjp(geglu, gate_up)
    hidden_low = hidden.astype(jnp.bfloat16)
    result = middle + jnp.dot(hidden_low, full_down, preferred_element_type=jnp.float32)
    grad_result = cotangent[0]
    grad_down_local = matmul_left(hidden_low, grad_result)
    grad_hidden = matmul_right(grad_result, full_down)
    grad_gate_up = geglu_back(grad_hidden)[0].astype(jnp.bfloat16)
    grad_in_local = matmul_left(normed_mlp_low, grad_gate_up)
    grad_normed_mlp = matmul_right(grad_gate_up, full_in)
    grad_middle_norm, grad_gain_second = mlp_norm_back(grad_normed_mlp)
    grad_middle = grad_result.astype(jnp.float32) + grad_middle_norm
    grad_branch = grad_middle.astype(jnp.bfloat16)
    grad_out_local = matmul_left(attended_low, grad_branch)
    grad_attended = (
        matmul_right(grad_branch, full_out).reshape(count, HEADS, HEAD_DIM).astype(jnp.bfloat16)
    )
    probs = jnp.exp(score_table() - logsum)
    probs_low = probs.astype(jnp.bfloat16)
    grad_probs = jnp.einsum(
        "qhd,khd->hqk", grad_attended, values_wide, preferred_element_type=jnp.float32
    )
    row_dot = jnp.sum(probs * grad_probs, axis=-1, keepdims=True)
    grad_scores = (probs * (grad_probs - row_dot)).astype(jnp.bfloat16)
    grad_query = (
        jnp.einsum("hqk,khd->qhd", grad_scores, keys_wide, preferred_element_type=jnp.float32)
        * scale
    )
    grad_keys_wide = (
        jnp.einsum("hqk,qhd->khd", grad_scores, query_low, preferred_element_type=jnp.float32)
        * scale
    )
    grad_values_wide = jnp.einsum(
        "hqk,qhd->khd", probs_low, grad_attended, preferred_element_type=jnp.float32
    )
    grad_wide = jnp.concatenate(
        [grad_keys_wide.reshape(extent, D), grad_values_wide.reshape(extent, D)], axis=1
    )
    lanes = lax.axis_size("seq")
    above = lax.ppermute(
        grad_wide[extent - HALF_WINDOW :].astype(jnp.bfloat16),
        "seq",
        [(i, i + 1) for i in range(lanes - 1)],
    )
    below = lax.ppermute(
        grad_wide[:HALF_WINDOW].astype(jnp.bfloat16),
        "seq",
        [(i + 1, i) for i in range(lanes - 1)],
    )
    returned = jnp.concatenate([above, below], axis=0).astype(jnp.float32)
    grad_own = grad_wide[HALF_WINDOW : HALF_WINDOW + count] + returned
    grad_key = key_back(grad_own[:, :D].reshape(count, HEADS, HEAD_DIM))[0]
    grad_q = query_back(grad_query)[0]
    grad_mixed = jnp.concatenate(
        [grad_q.reshape(count, D), grad_key.reshape(count, D), grad_own[:, D:]], axis=1
    ).astype(jnp.bfloat16)
    grad_qkv_local = matmul_left(normed_low, grad_mixed)
    grad_normed = matmul_right(grad_mixed, full_qkv)
    grad_tokens_norm, grad_gain_first = norm_back(grad_normed)
    grad_tokens = grad_middle + grad_tokens_norm
    if lanes == 8:
        gain_rows = jnp.concatenate(
            [grad_gain_first.reshape(4, 1, held), grad_gain_second.reshape(4, 1, held)], axis=2
        )
        gain_rows = jnp.pad(gain_rows, ((0, 0), (0, PAD - 1), (0, D - 2 * held)))
        hidden_rows = jnp.pad(
            hidden_low.T.reshape(4, owned_rows, count), ((0, 0), (0, PAD), (0, 0))
        )
        grad_qkv, grad_out, grad_in, packed = reduce_grads(
            [normed_low.T, attended_low.T, normed_mlp_low.T, hidden_rows.reshape(-1, count)],
            [grad_mixed, grad_branch, grad_gate_up, grad_result],
            gain_rows.astype(jnp.bfloat16),
        )
        return (
            result[None].astype(jnp.bfloat16),
            grad_tokens[None],
            grad_qkv,
            grad_out,
            grad_in,
            packed[:owned_rows],
            packed[owned_rows, :held],
            packed[owned_rows, held : 2 * held],
        )
    owned = (
        lax.psum_scatter(
            grad_qkv_local.astype(jnp.bfloat16), "fsdp", scatter_dimension=0, tiled=True
        ).astype(jnp.float32),
        lax.psum_scatter(
            grad_out_local.astype(jnp.bfloat16), "fsdp", scatter_dimension=0, tiled=True
        ).astype(jnp.float32),
        lax.psum_scatter(
            grad_in_local.astype(jnp.bfloat16), "fsdp", scatter_dimension=0, tiled=True
        ).astype(jnp.float32),
        lax.psum_scatter(
            grad_down_local.astype(jnp.bfloat16), "fsdp", scatter_dimension=0, tiled=True
        ).astype(jnp.float32),
        lax.psum_scatter(
            grad_gain_first.astype(jnp.bfloat16), "fsdp", scatter_dimension=0, tiled=True
        ).astype(jnp.float32),
        lax.psum_scatter(
            grad_gain_second.astype(jnp.bfloat16), "fsdp", scatter_dimension=0, tiled=True
        ).astype(jnp.float32),
    )
    owned_flat = pack_rows(owned, 1)
    owned_share = owned_flat.shape[1] // lanes
    lane_part = lax.psum_scatter(
        owned_flat.reshape(lanes, owned_share), "seq", scatter_dimension=0, tiled=True
    )
    summed_row = (
        lax.all_gather(lane_part.astype(jnp.bfloat16), "seq", axis=0, tiled=True)
        .astype(lane_part.dtype)
        .reshape(-1)
    )
    grad_qkv, grad_out, grad_in, grad_down, grad_gain_attn, grad_gain_mlp = unpack_row(
        summed_row, owned, 1
    )
    return (
        result[None].astype(jnp.bfloat16),
        grad_tokens[None],
        grad_qkv,
        grad_out,
        grad_in,
        grad_down,
        grad_gain_attn,
        grad_gain_mlp,
    )


def solution(mesh):
    in_specs = (
        P("fsdp", "seq", None),
        P("fsdp", "seq"),
        P("fsdp", "seq", None),
        P("fsdp", None),
        P("fsdp", None),
        P("fsdp", None),
        P("fsdp", None),
        P("fsdp"),
        P("fsdp"),
    )
    out_specs = (
        P("fsdp", "seq", None),
        P("fsdp", "seq", None),
        P("fsdp", None),
        P("fsdp", None),
        P("fsdp", None),
        P("fsdp", None),
        P("fsdp"),
        P("fsdp"),
    )
    return jax.shard_map(
        on_device, mesh=mesh, in_specs=in_specs, out_specs=out_specs, check_vma=False
    )
```

```python
import functools
import math

import jax
import jax.numpy as jnp
from jax import lax
from jax.experimental import pallas as pl
from jax.experimental.pallas import tpu as pltpu
from jax.sharding import PartitionSpec as P

D = 768
HEADS = 12
HEAD_DIM = 64
FF = 1152
HALF_WINDOW = 64


eps = 1e-05
rope_base = 10000.0
masked_score = -1e30


def layer_norm(values, gain):
    center = values - jnp.mean(values, axis=-1, keepdims=True)
    spread = jnp.mean(center * center, axis=-1, keepdims=True)
    return center * lax.rsqrt(spread + eps) * gain


def matmul_left(left, right):
    return lax.dot_general(
        left, right, (((0,), (0,)), ((), ())), preferred_element_type=jnp.float32
    )


def matmul_right(left, right):
    return lax.dot_general(
        left, right, (((1,), (1,)), ((), ())), preferred_element_type=jnp.float32
    )


def pack_rows(pieces, groups):
    joined = jnp.concatenate([piece.reshape(groups, -1) for piece in pieces], axis=1)
    return joined


def unpack_row(flat_row, pieces, groups):
    results = []
    offset = 0
    for piece in pieces:
        shape = (piece.shape[0] // groups,) + piece.shape[1:]
        size = math.prod(shape)
        results.append(flat_row[offset : offset + size].reshape(shape))
        offset = offset + size
    return results


MESH = pl.DeviceIdType.MESH
PAD = 32
SHARES = ((48, 1152), (48, 384), (48, 1152), (80, 384))
BIT1_FIRST = (True, True, False, False)


def partner(me, step):
    return me + step * (1 - 2 * ((me // step) % 2))


def place():
    me, z = lax.axis_index("seq"), lax.axis_index("fsdp")
    core, b1, b2 = me % 2, (me // 2) % 2, (me // 4) % 2
    return me, z, core, b1, b2


def greet(me, z):
    barrier = pltpu.get_barrier_semaphore()
    for step in (1, 2, 4):
        pl.semaphore_signal(
            barrier, inc=1, device_id={"seq": partner(me, step)}, device_id_type=MESH
        )
    for step in (1, 2, 3):
        pl.semaphore_signal(
            barrier, inc=1, device_id={"fsdp": (z + step) % 4}, device_id_type=MESH
        )
    pl.semaphore_wait(barrier, 6)


def rows(block, size, count=1):
    return pl.ds(pl.multiple_of(block * size, 16), size * count)


def cols(half, size):
    return pl.ds(pl.multiple_of(half * size, 128), size)


def push(src, dst, send, recv, target):
    return pltpu.make_async_remote_copy(
        src_ref=src, dst_ref=dst, send_sem=send, recv_sem=recv,
        device_id=target, device_id_type=MESH,
    )


def gather_order():
    order = []
    for k in range(4):
        if k < 3:
            order += [(0, k, w) for w in range(4)]
        if k > 0:
            order += [(2, k - 1, w) for w in range(4)]
        if k < 3:
            order += [(1, k, w) for w in range(4)]
    return order


def gather_kernel(*refs):
    ins, outs = refs[:4], refs[4:8]
    local, zs, zr, fs, s1, r1, s2, r2, s3, r3 = refs[8:]
    me, z, core, b1, b2 = place()
    quarter = b1 + 2 * b2
    greet(me, z)
    inner = (z == 1) | (z == 2)
    sent = []
    own = []
    for w, (r, c) in enumerate(SHARES):
        src = ins[w].at[rows(quarter, r), cols(core, c)]
        dst = outs[w].at[z, rows(quarter, r), cols(core, c)]
        up = push(src, dst, zs.at[w, 0], zr.at[w, z], {"fsdp": lax.rem(z + 1, 4)})
        down = push(src, dst, zs.at[w, 1], zr.at[w, z], {"fsdp": lax.rem(z + 3, 4)})
        own.append((up, down))
        pl.when(z < 3)(up.start)
        pl.when(z > 0)(down.start)
    copies = []
    for w in range(4):
        copy = pltpu.make_async_copy(ins[w], outs[w].at[z], local.at[w])
        copy.start()
        copies.append(copy)
    first = (z + 3) % 4 - 2 * ((3 - z) // 3)
    last = 3 * (1 - z // 2)
    second = 6 - z - first - last
    origins = (first, second, last)
    onward = ((z + 1) % 4, (z + 3) % 4, (3 * z + 1) % 4)
    events = [(k, w) for k in range(3) for w in range(4)]
    forwards, stage1, stage2, stage3 = {}, {}, {}, {}

    def arrive(k, w):
        r, c = SHARES[w]
        o = origins[k]
        mine = outs[w].at[o, rows(quarter, r), cols(core, c)]
        forward = push(mine, mine, fs.at[w, k], zr.at[w, o], {"fsdp": onward[k]})
        forwards[k, w] = forward
        forward.wait_recv()
        pl.when(inner)(forward.start)
        step = 2 if BIT1_FIRST[w] else 4
        copy = push(mine, mine, s1.at[w, k], r1.at[w, k], {"seq": partner(me, step)})
        copy.start()
        stage1[k, w] = copy

    def pair(k, w):
        r, c = SHARES[w]
        o = origins[k]
        stage1[k, w].wait_recv()
        half = cols(core, c)
        if BIT1_FIRST[w]:
            blocks = [outs[w].at[o, rows(2 * b2, r, 2), half]]
            step = 4
        else:
            blocks = [outs[w].at[o, rows(b1 + 2 * j, r), half] for j in range(2)]
            step = 2
        stage2[k, w] = []
        for j, block in enumerate(blocks):
            copy = push(block, block, s2.at[w, k, j], r2.at[w, k, j], {"seq": partner(me, step)})
            copy.start()
            stage2[k, w].append(copy)

    def across(k, w):
        r, c = SHARES[w]
        for copy in stage2[k, w]:
            copy.wait_recv()
        block = outs[w].at[origins[k], :, cols(core, c)]
        copy = push(block, block, s3.at[w, k], r3.at[w, k], {"seq": partner(me, 1)})
        copy.start()
        stage3[k, w] = copy

    acts = (arrive, pair, across)
    for act, k, w in gather_order():
        acts[act](k, w)
    for event in events:
        stage3[event].wait_recv()
    for copy in copies:
        copy.wait()
    for up, down in own:
        pl.when(z < 3)(up.wait_send)
        pl.when(z > 0)(down.wait_send)
    for event in events:
        pl.when(inner)(forwards[event].wait_send)
        stage1[event].wait_send()
        for copy in stage2[event]:
            copy.wait_send()
        stage3[event].wait_send()


def gather_weights(shards):
    sem = pltpu.SemaphoreType.DMA
    return pl.pallas_call(
        gather_kernel,
        out_shape=[jax.ShapeDtypeStruct((4, 4 * r, 2 * c), jnp.bfloat16) for r, c in SHARES],
        in_specs=[pl.BlockSpec(memory_space=pltpu.VMEM)] * 4,
        out_specs=[pl.BlockSpec(memory_space=pl.ANY)] * 4,
        scratch_shapes=[
            sem((4,)), sem((4, 2)), sem((4, 4)), sem((4, 3)), sem((4, 3)), sem((4, 3)),
            sem((4, 3, 2)), sem((4, 3, 2)), sem((4, 3)), sem((4, 3)),
        ],
        compiler_params=pltpu.CompilerParams(
            collective_id=0, has_side_effects=True, vmem_limit_bytes=32 * 1024 * 1024
        ),
    )(*shards)


WIDE = 384
CHUNKS = ((2, 0), (0, 0), (2, 384), (0, 384), (2, 768), (0, 768), (3, 0), (1, 0))


def reduce_order():
    ahead = 4
    order = [("first", p) for p in range(ahead)]
    for t in range(4 + 6):
        for act, lag in (
            ("finish", 6), ("across", 5), ("spread", 4), ("owner", 3), ("share", 2), ("pair", 0)
        ):
            if 0 <= t - lag < 4:
                order.append((act, t - lag))
        if t + ahead < 4:
            order.append(("first", t + ahead))
    return order


def reduce_kernel(*refs):
    xin, yin, gin, outs = refs[:4], refs[4:8], refs[8], refs[9:14]
    xb, yb, gb = refs[14:18], refs[18:22], refs[22]
    cs, b1s, s1s, b2s, s2s, bz, ag = (refs[23 + 8 * i : 31 + 8 * i] for i in range(7))
    csem, sem1, sem2, zsem, asem = refs[79:]
    me, z, core, b1, b2 = place()
    quarter = b1 + 2 * b2
    greet(me, z)
    f32, low = jnp.float32, jnp.bfloat16
    sent = []
    table = {}

    def go(key, src, dst, sems, target):
        copy = push(src, dst, sems.at[0], sems.at[1], target)
        copy.start()
        sent.append(copy)
        table.setdefault(key, []).append(copy)

    def take(key):
        for copy in table[key]:
            copy.wait_recv()

    twin = {"seq": partner(me, 1)}
    lanes = cols(core, 128)
    for w in (2, 0, 3, 1):
        c = SHARES[w][1]
        go(("x", w), xin[w], xb[w].at[:, lanes], csem.at[0, w], twin)
        go(("x", w), yin[w].at[:, cols(1 - core, c)], yb[w].at[rows(core, 128)], csem.at[1, w], twin)
    go("g", gin.at[:, :, cols(1 - core, WIDE)], gb, csem.at[2, 0], twin)
    for w in (2, 0, 3, 1):
        xb[w][:, lanes] = xin[w][...]
        yb[w][rows(core, 128), :] = yin[w][:, cols(core, SHARES[w][1])]

    def product(i):
        w, start = CHUNKS[i]
        height = 4 * SHARES[w][0]
        if start == 0:
            take(("x", w))

        def body(o, carry):
            left = xb[w][pl.ds(pl.multiple_of(o * height, 16), height), :]
            right = yb[w][:, start : start + WIDE]
            cs[i][o] = jnp.dot(left, right, preferred_element_type=f32).astype(low)
            return carry

        lax.fori_loop(0, 4, body, 0)
        if w == 3:
            take("g")
            mine = gin[:, :, cols(core, WIDE)].astype(f32)
            cs[i][:, height - PAD :, :] = (mine + gb[...].astype(f32)).astype(low)

    def first(i):
        product(i)
        w = CHUNKS[i][0]
        r = SHARES[w][0]
        if BIT1_FIRST[w]:
            src = cs[i].at[:, rows(2 * (1 - b2), r, 2), :]
            go((1, i), src, b1s[i], sem1.at[i, 0], {"seq": partner(me, 4)})
        else:
            for j in range(2):
                src = cs[i].at[:, rows(1 - b1 + 2 * j, r), :]
                dst = b1s[i].at[:, pl.ds(j * r, r), :]
                go((1, i), src, dst, sem1.at[i, j], {"seq": partner(me, 2)})

    def pair(i):
        w = CHUNKS[i][0]
        r = SHARES[w][0]
        take((1, i))

        def body(t, carry):
            o, j = t // 2, t % 2
            block = 2 * b2 + j if BIT1_FIRST[w] else b1 + 2 * j
            there = pl.ds(pl.multiple_of(j * r, 16), r)
            mine = cs[i][o, rows(block, r), :].astype(f32)
            s1s[i][o, there, :] = (mine + b1s[i][o, there, :].astype(f32)).astype(low)
            return carry

        lax.fori_loop(0, 8, body, 0)
        bit, step = (b1, 2) if BIT1_FIRST[w] else (b2, 4)
        src = s1s[i].at[:, rows(1 - bit, r), :]
        go((2, i), src, b2s[i], sem2.at[i], {"seq": partner(me, step)})

    def share(i):
        w = CHUNKS[i][0]
        r = SHARES[w][0]
        take((2, i))
        bit = b1 if BIT1_FIRST[w] else b2

        def body(o, carry):
            mine = s1s[i][o, rows(bit, r), :].astype(f32)
            s2s[i][o] = (mine + b2s[i][o].astype(f32)).astype(low)
            return carry

        lax.fori_loop(0, 4, body, 0)
        for d in (2, 1, 3):
            to = (z + d) % 4
            go((3, i), s2s[i].at[to], bz[i].at[d - 1], zsem.at[i, d - 1], {"fsdp": to})

    def owner(i):
        w = CHUNKS[i][0]
        r = SHARES[w][0]
        take((3, i))
        total = s2s[i][z].astype(f32)
        for d in range(3):
            total = total + bz[i][d].astype(f32)
        ag[i][core, rows(quarter, r), :] = total.astype(low)
        block = ag[i].at[core, rows(quarter, r), :]
        step = 2 if BIT1_FIRST[w] else 4
        go((4, i), block, block, asem.at[i, 0], {"seq": partner(me, step)})

    def spread(i):
        w = CHUNKS[i][0]
        r = SHARES[w][0]
        take((4, i))
        if BIT1_FIRST[w]:
            block = ag[i].at[core, rows(2 * b2, r, 2), :]
            go((5, i), block, block, asem.at[i, 1], {"seq": partner(me, 4)})
        else:
            for j in range(2):
                block = ag[i].at[core, rows(b1 + 2 * j, r), :]
                go((5, i), block, block, asem.at[i, 1 + j], {"seq": partner(me, 2)})

    def across(i):
        take((5, i))
        block = ag[i].at[core]
        go((6, i), block, block, asem.at[i, 3], twin)

    def finish(i):
        w, start = CHUNKS[i]
        r, c = SHARES[w]
        take((6, i))

        def body(t, carry):
            part = pl.ds(pl.multiple_of(t * r, 16), r)
            for half in range(2):
                at = half * c + start
                outs[w][part, at : at + WIDE] = ag[i][half, part, :].astype(f32)
            return carry

        if w < 3:
            lax.fori_loop(0, 4, body, 0)
            return
        lax.fori_loop(0, 3, body, 0)
        for half in range(2):
            at = half * c
            for to, begin, end in ((3, 3 * r, 4 * r - PAD), (4, 4 * r - PAD, 4 * r)):
                low_row = begin if to == 3 else 0
                part = ag[i][half, begin:end, :].astype(f32)
                outs[to][low_row : low_row + end - begin, at : at + WIDE] = part

    acts = {
        "first": first, "pair": pair, "share": share, "owner": owner,
        "spread": spread, "across": across, "finish": finish,
    }
    for act, p in reduce_order():
        for i in (2 * p, 2 * p + 1):
            acts[act](i)
    for copy in sent:
        copy.wait_send()


def reduce_grads(lefts, rights, gain_rows):
    sem = pltpu.SemaphoreType.DMA
    vmem = lambda *shape: pltpu.VMEM(shape, jnp.bfloat16)
    heights = [SHARES[w][0] for w, start in CHUNKS]
    count = len(CHUNKS)
    shapes = [(4 * r, 2 * c) for r, c in SHARES]
    shapes = shapes[:3] + [(shapes[3][0] - PAD, shapes[3][1]), (PAD, shapes[3][1])]
    return pl.pallas_call(
        reduce_kernel,
        out_shape=[jax.ShapeDtypeStruct(shape, jnp.float32) for shape in shapes],
        in_specs=[pl.BlockSpec(memory_space=pltpu.VMEM)] * 9,
        out_specs=[pl.BlockSpec(memory_space=pltpu.VMEM)] * 5,
        scratch_shapes=[vmem(16 * r, 256) for r, c in SHARES]
        + [vmem(256, c) for r, c in SHARES]
        + [vmem(4, PAD, WIDE)]
        + [vmem(4, 4 * r, WIDE) for r in heights]
        + [vmem(4, 2 * r, WIDE) for r in heights] * 2
        + [vmem(4, r, WIDE) for r in heights] * 2
        + [vmem(3, r, WIDE) for r in heights]
        + [vmem(2, 4 * r, WIDE) for r in heights]
        + [
            sem((3, 4, 2)), sem((count, 2, 2)), sem((count, 2)), sem((count, 3, 2)),
            sem((count, 4, 2)),
        ],
        compiler_params=pltpu.CompilerParams(
            collective_id=1, has_side_effects=True, vmem_limit_bytes=56 * 1024 * 1024
        ),
    )(*lefts, *rights, gain_rows)


def swap_halves(values):
    lane = lax.broadcasted_iota(jnp.int32, values.shape, 1)
    return jnp.where(lane % 64 < 32, pltpu.roll(values, 96, 1), pltpu.roll(values, 32, 1))


def turn_kernel(mixed, cosine, sine, flags, q_out, kv_out):
    cos, sin = cosine[...], sine[...]
    for g in range(2 * D // 128):
        u = mixed[:, 128 * g : 128 * g + 128]
        turned = (u * cos + swap_halves(u) * sin).astype(jnp.bfloat16)
        if g < D // 128:
            q_out[:, 128 * g : 128 * g + 128] = turned
        else:
            at = 128 * g - D
            kv_out[:, at : at + 128] = turned
    kv_out[:, D : 2 * D] = mixed[:, 2 * D :].astype(jnp.bfloat16)
    kv_out[:, 2 * D :] = jnp.broadcast_to(flags[...], (flags.shape[0], 128)).astype(jnp.bfloat16)


def widen(above, own, below, start, size):
    return jnp.concatenate([ref[:, start : start + size] for ref in (above, own, below)], axis=0)


def visible(above, own, below, pos):
    flag = widen(above, own, below, 2 * D, 128).astype(jnp.float32).T
    shape = flag.shape
    offset = (
        lax.broadcasted_iota(jnp.int32, shape, 1)
        - HALF_WINDOW
        - lax.broadcasted_iota(jnp.int32, shape, 0)
    ).astype(jnp.float32)
    place_of = jnp.broadcast_to(pos[...], shape)
    earlier = (offset >= 0.0) | (place_of >= -offset)
    later = (offset < 0.0) | (flag - 1.0 >= offset)
    return (jnp.abs(offset) <= HALF_WINDOW) & (flag > 0.5) & earlier & later


def dot_rows(left, right):
    return lax.dot_general(
        left, right, (((1,), (1,)), ((), ())), preferred_element_type=jnp.float32
    )


def attend_kernel(q, above, own, below, pos, o_out, lse_out):
    allowed = visible(above, own, below, pos)
    scale = HEAD_DIM ** (-0.5)
    lane = lax.broadcasted_iota(jnp.int32, lse_out.shape, 1)
    kept = jnp.zeros(lse_out.shape, jnp.float32)
    for g in range(HEADS // 2):
        keys = widen(above, own, below, 128 * g, 128)
        values = widen(above, own, below, D + 128 * g, 128)
        queries = q[:, 128 * g : 128 * g + 128]
        outs = []
        for j in range(2):
            part = slice(64 * j, 64 * j + 64)
            scores = dot_rows(queries[:, part], keys[:, part]) * scale
            scores = jnp.where(allowed, scores, masked_score)
            top = jnp.max(scores, axis=-1, keepdims=True)
            expo = jnp.exp(scores - top)
            total = jnp.sum(expo, axis=-1, keepdims=True)
            kept = jnp.where(lane == 2 * g + j, top + jnp.log(total), kept)
            probs = (expo / total).astype(jnp.bfloat16)
            outs.append(jnp.dot(probs, values[:, part], preferred_element_type=jnp.float32))
        o_out[:, 128 * g : 128 * g + 128] = jnp.concatenate(outs, axis=1).astype(jnp.bfloat16)
    lse_out[...] = kept


def attend_back_kernel(
    q, above, own, below, pos, grad, lse, cosine, sine, dq_out, up_out, mid_out, down_out
):
    allowed = visible(above, own, below, pos)
    scale = HEAD_DIM ** (-0.5)
    cos, sin = cosine[...], sine[...]
    low = jnp.bfloat16
    count = q.shape[0]
    edge = count + HALF_WINDOW
    for g in range(HEADS // 2):
        at = slice(128 * g, 128 * g + 128)
        keys = widen(above, own, below, 128 * g, 128)
        values = widen(above, own, below, D + 128 * g, 128)
        queries, grads = q[:, at], grad[:, at]
        dqs, dks, dvs = [], [], []
        for j in range(2):
            part = slice(64 * j, 64 * j + 64)
            head = 2 * g + j
            scores = dot_rows(queries[:, part], keys[:, part]) * scale
            scores = jnp.where(allowed, scores, masked_score)
            probs = jnp.exp(scores - lse[:, head : head + 1])
            probs_low = probs.astype(low)
            dp = dot_rows(grads[:, part], values[:, part])
            row = jnp.sum(probs * dp, axis=-1, keepdims=True)
            ds = (probs * (dp - row)).astype(low)
            dqs.append(jnp.dot(ds, keys[:, part], preferred_element_type=jnp.float32) * scale)
            dks.append(matmul_left(ds, queries[:, part]) * scale)
            dvs.append(matmul_left(probs_low, grads[:, part]))
        dq = jnp.concatenate(dqs, axis=1)
        dq_out[:, at] = (dq * cos - swap_halves(dq) * sin).astype(low)
        for start, pieces in ((0, dks), (D, dvs)):
            wide = jnp.concatenate(pieces, axis=1)
            to = slice(start + 128 * g, start + 128 * g + 128)
            up_out[:, to] = wide[:HALF_WINDOW].astype(low)
            mid_out[:, to] = wide[HALF_WINDOW:edge]
            down_out[:, to] = wide[edge:].astype(low)


def join_kernel(dq, mid, above, below, cosine, sine, out):
    cos, sin = cosine[...], sine[...]
    out[:, :D] = dq[...]
    for g in range(2 * D // 128):
        at = slice(128 * g, 128 * g + 128)
        back = jnp.concatenate([above[:, at], below[:, at]], axis=0).astype(jnp.float32)
        total = mid[:, at] + back
        if g < D // 128:
            total = total * cos - swap_halves(total) * sin
        out[:, D + 128 * g : D + 128 * g + 128] = total.astype(jnp.bfloat16)


def local_call(kernel, shapes, *operands):
    vmem = pl.BlockSpec(memory_space=pltpu.VMEM)
    return pl.pallas_call(
        kernel,
        out_shape=[jax.ShapeDtypeStruct(shape, kind) for shape, kind in shapes],
        in_specs=[vmem] * len(operands),
        out_specs=[vmem] * len(shapes),
        compiler_params=pltpu.CompilerParams(vmem_limit_bytes=32 * 1024 * 1024),
    )(*operands)


def neighbours(up, down):
    lanes = lax.axis_size("seq")
    above = lax.ppermute(down, "seq", [(i, i + 1) for i in range(lanes - 1)])
    below = lax.ppermute(up, "seq", [(i + 1, i) for i in range(lanes - 1)])
    return above, below


def on_device(inputs, positions, cotangent, w_qkv, w_out, w_in, w_down, gain_attn, gain_mlp):
    gains = jnp.concatenate([gain_attn, gain_mlp])
    gains = jnp.pad(gains[None], ((0, PAD - 1), (0, D - gains.shape[0])))
    packed = jnp.concatenate([w_down, gains], axis=0)
    full_qkv, full_out, full_in, full_packed = gather_weights([w_qkv, w_out, w_in, packed])
    full_qkv = full_qkv.reshape(D, 3 * D)
    full_out = full_out.reshape(D, D)
    full_in = full_in.reshape(D, 2 * FF)
    owned_rows = w_down.shape[0]
    full_down = full_packed[:, :owned_rows].reshape(FF, D)
    held = gain_attn.shape[0]
    gain_first = full_packed[:, owned_rows, :held].reshape(D).astype(jnp.float32)
    gain_second = full_packed[:, owned_rows, held : 2 * held].reshape(D).astype(jnp.float32)
    tokens = inputs[0].astype(jnp.float32)
    token_pos = positions[0]
    count = tokens.shape[0]
    normed, norm_back = jax.vjp(layer_norm, tokens, gain_first)
    normed_low = normed.astype(jnp.bfloat16)
    mixed = jnp.dot(normed_low, full_qkv, preferred_element_type=jnp.float32)
    half = HEAD_DIM // 2
    ladder = jnp.arange(half).astype(jnp.float32) * (2.0 / HEAD_DIM)
    angles = token_pos.astype(jnp.float32)[:, None] * (rope_base ** (-ladder))[None, :]
    cosine, sine = jnp.cos(angles), jnp.sin(angles)
    cosine = jnp.concatenate([cosine] * 4, axis=1)
    sine = jnp.concatenate([-sine, sine] * 2, axis=1)
    flags = (jnp.minimum(token_pos, 127) + 1).astype(jnp.float32)[:, None]
    pos = token_pos.astype(jnp.float32)[:, None]
    low = jnp.bfloat16
    query_low, key_value = local_call(
        turn_kernel, [((count, D), low), ((count, 2 * D + 128), low)], mixed, cosine, sine, flags
    )
    above, below = neighbours(key_value[:HALF_WINDOW], key_value[count - HALF_WINDOW :])
    attended_low, logsum = local_call(
        attend_kernel,
        [((count, D), low), ((count, 128), jnp.float32)],
        query_low, above, key_value, below, pos,
    )
    middle = tokens + jnp.dot(attended_low, full_out, preferred_element_type=jnp.float32)
    normed_mlp, mlp_norm_back = jax.vjp(layer_norm, middle, gain_second)
    normed_mlp_low = normed_mlp.astype(jnp.bfloat16)
    gate_up = jnp.dot(normed_mlp_low, full_in, preferred_element_type=jnp.float32)

    def geglu(paired):
        return jax.nn.gelu(paired[:, :FF], approximate=False) * paired[:, FF:]

    hidden, geglu_back = jax.vjp(geglu, gate_up)
    hidden_low = hidden.astype(jnp.bfloat16)
    result = middle + jnp.dot(hidden_low, full_down, preferred_element_type=jnp.float32)
    grad_result = cotangent[0]
    grad_down_local = matmul_left(hidden_low, grad_result)
    grad_hidden = matmul_right(grad_result, full_down)
    grad_gate_up = geglu_back(grad_hidden)[0].astype(jnp.bfloat16)
    grad_in_local = matmul_left(normed_mlp_low, grad_gate_up)
    grad_normed_mlp = matmul_right(grad_gate_up, full_in)
    grad_middle_norm, grad_gain_second = mlp_norm_back(grad_normed_mlp)
    grad_middle = grad_result.astype(jnp.float32) + grad_middle_norm
    grad_branch = grad_middle.astype(jnp.bfloat16)
    grad_out_local = matmul_left(attended_low, grad_branch)
    grad_attended = matmul_right(grad_branch, full_out).astype(low)
    grad_query, up, own, down = local_call(
        attend_back_kernel,
        [
            ((count, D), low),
            ((HALF_WINDOW, 2 * D), low),
            ((count, 2 * D), jnp.float32),
            ((HALF_WINDOW, 2 * D), low),
        ],
        query_low, above, key_value, below, pos, grad_attended, logsum, cosine, sine,
    )
    back_above, back_below = neighbours(up, down)
    (grad_mixed,) = local_call(
        join_kernel, [((count, 3 * D), low)], grad_query, own, back_above, back_below, cosine, sine
    )
    grad_qkv_local = matmul_left(normed_low, grad_mixed)
    grad_normed = matmul_right(grad_mixed, full_qkv)
    grad_tokens_norm, grad_gain_first = norm_back(grad_normed)
    grad_tokens = grad_middle + grad_tokens_norm
    lanes = lax.axis_size("seq")
    if lanes == 8:
        gain_rows = jnp.concatenate(
            [grad_gain_first.reshape(4, 1, held), grad_gain_second.reshape(4, 1, held)], axis=2
        )
        gain_rows = jnp.pad(gain_rows, ((0, 0), (0, PAD - 1), (0, D - 2 * held)))
        hidden_rows = jnp.pad(
            hidden_low.T.reshape(4, owned_rows, count), ((0, 0), (0, PAD), (0, 0))
        )
        grad_qkv, grad_out, grad_in, grad_down, gain_sums = reduce_grads(
            [normed_low.T, attended_low.T, normed_mlp_low.T, hidden_rows.reshape(-1, count)],
            [grad_mixed, grad_branch, grad_gate_up, grad_result],
            gain_rows.astype(jnp.bfloat16),
        )
        return (
            result[None].astype(jnp.bfloat16),
            grad_tokens[None],
            grad_qkv,
            grad_out,
            grad_in,
            grad_down,
            gain_sums[0, :held],
            gain_sums[0, held : 2 * held],
        )
    owned = (
        lax.psum_scatter(
            grad_qkv_local.astype(jnp.bfloat16), "fsdp", scatter_dimension=0, tiled=True
        ).astype(jnp.float32),
        lax.psum_scatter(
            grad_out_local.astype(jnp.bfloat16), "fsdp", scatter_dimension=0, tiled=True
        ).astype(jnp.float32),
        lax.psum_scatter(
            grad_in_local.astype(jnp.bfloat16), "fsdp", scatter_dimension=0, tiled=True
        ).astype(jnp.float32),
        lax.psum_scatter(
            grad_down_local.astype(jnp.bfloat16), "fsdp", scatter_dimension=0, tiled=True
        ).astype(jnp.float32),
        lax.psum_scatter(
            grad_gain_first.astype(jnp.bfloat16), "fsdp", scatter_dimension=0, tiled=True
        ).astype(jnp.float32),
        lax.psum_scatter(
            grad_gain_second.astype(jnp.bfloat16), "fsdp", scatter_dimension=0, tiled=True
        ).astype(jnp.float32),
    )
    owned_flat = pack_rows(owned, 1)
    owned_share = owned_flat.shape[1] // lanes
    lane_part = lax.psum_scatter(
        owned_flat.reshape(lanes, owned_share), "seq", scatter_dimension=0, tiled=True
    )
    summed_row = (
        lax.all_gather(lane_part.astype(jnp.bfloat16), "seq", axis=0, tiled=True)
        .astype(lane_part.dtype)
        .reshape(-1)
    )
    grad_qkv, grad_out, grad_in, grad_down, grad_gain_attn, grad_gain_mlp = unpack_row(
        summed_row, owned, 1
    )
    return (
        result[None].astype(jnp.bfloat16),
        grad_tokens[None],
        grad_qkv,
        grad_out,
        grad_in,
        grad_down,
        grad_gain_attn,
        grad_gain_mlp,
    )


def solution(mesh):
    in_specs = (
        P("fsdp", "seq", None),
        P("fsdp", "seq"),
        P("fsdp", "seq", None),
        P("fsdp", None),
        P("fsdp", None),
        P("fsdp", None),
        P("fsdp", None),
        P("fsdp"),
        P("fsdp"),
    )
    out_specs = (
        P("fsdp", "seq", None),
        P("fsdp", "seq", None),
        P("fsdp", None),
        P("fsdp", None),
        P("fsdp", None),
        P("fsdp", None),
        P("fsdp"),
        P("fsdp"),
    )
    return jax.shard_map(
        on_device, mesh=mesh, in_specs=in_specs, out_specs=out_specs, check_vma=False
    )
```

```python
import functools
import math

import jax
import jax.numpy as jnp
from jax import lax
from jax.experimental import pallas as pl
from jax.experimental.pallas import tpu as pltpu
from jax.sharding import PartitionSpec as P

D = 768
HEADS = 12
HEAD_DIM = 64
FF = 1152
HALF_WINDOW = 64


eps = 1e-05
rope_base = 10000.0
masked_score = -1e30


def layer_norm(values, gain):
    center = values - jnp.mean(values, axis=-1, keepdims=True)
    spread = jnp.mean(center * center, axis=-1, keepdims=True)
    return center * lax.rsqrt(spread + eps) * gain


def matmul_left(left, right):
    return lax.dot_general(
        left, right, (((0,), (0,)), ((), ())), preferred_element_type=jnp.float32
    )


def matmul_right(left, right):
    return lax.dot_general(
        left, right, (((1,), (1,)), ((), ())), preferred_element_type=jnp.float32
    )


def pack_rows(pieces, groups):
    joined = jnp.concatenate([piece.reshape(groups, -1) for piece in pieces], axis=1)
    return joined


def unpack_row(flat_row, pieces, groups):
    results = []
    offset = 0
    for piece in pieces:
        shape = (piece.shape[0] // groups,) + piece.shape[1:]
        size = math.prod(shape)
        results.append(flat_row[offset : offset + size].reshape(shape))
        offset = offset + size
    return results


MESH = pl.DeviceIdType.MESH
PAD = 32
SHARES = ((48, 1152), (48, 384), (48, 1152), (80, 384))
BIT1_FIRST = (True, True, False, False)


def partner(me, step):
    return me + step * (1 - 2 * ((me // step) % 2))


def place():
    me, z = lax.axis_index("seq"), lax.axis_index("fsdp")
    core, b1, b2 = me % 2, (me // 2) % 2, (me // 4) % 2
    return me, z, core, b1, b2


def greet(me, z, others=()):
    barrier = pltpu.get_barrier_semaphore()
    for other in others:
        pl.semaphore_signal(barrier, inc=1, device_id={"seq": other}, device_id_type=MESH)
    for step in (1, 2, 4):
        pl.semaphore_signal(
            barrier, inc=1, device_id={"seq": partner(me, step)}, device_id_type=MESH
        )
    for step in (1, 2, 3):
        pl.semaphore_signal(
            barrier, inc=1, device_id={"fsdp": (z + step) % 4}, device_id_type=MESH
        )
    pl.semaphore_wait(barrier, 6 + len(others))


def rows(block, size, count=1):
    return pl.ds(pl.multiple_of(block * size, 16), size * count)


def cols(half, size):
    return pl.ds(pl.multiple_of(half * size, 128), size)


def push(src, dst, send, recv, target):
    return pltpu.make_async_remote_copy(
        src_ref=src, dst_ref=dst, send_sem=send, recv_sem=recv,
        device_id=target, device_id_type=MESH,
    )


def gather_order():
    order = []
    for k in range(4):
        if k < 3:
            order += [(0, k, w) for w in range(4)]
        if k > 0:
            order += [(2, k - 1, w) for w in range(4)]
        if k < 3:
            order += [(1, k, w) for w in range(4)]
    return order


def gather_kernel(*refs):
    ins, outs = refs[:4], refs[4:8]
    local, zs, zr, fs, s1, r1, s2, r2, s3, r3 = refs[8:]
    me, z, core, b1, b2 = place()
    quarter = b1 + 2 * b2
    greet(me, z)
    inner = (z == 1) | (z == 2)
    sent = []
    own = []
    for w, (r, c) in enumerate(SHARES):
        src = ins[w].at[rows(quarter, r), cols(core, c)]
        dst = outs[w].at[z, rows(quarter, r), cols(core, c)]
        up = push(src, dst, zs.at[w, 0], zr.at[w, z], {"fsdp": lax.rem(z + 1, 4)})
        down = push(src, dst, zs.at[w, 1], zr.at[w, z], {"fsdp": lax.rem(z + 3, 4)})
        own.append((up, down))
        pl.when(z < 3)(up.start)
        pl.when(z > 0)(down.start)
    copies = []
    for w in range(4):
        copy = pltpu.make_async_copy(ins[w], outs[w].at[z], local.at[w])
        copy.start()
        copies.append(copy)
    first = (z + 3) % 4 - 2 * ((3 - z) // 3)
    last = 3 * (1 - z // 2)
    second = 6 - z - first - last
    origins = (first, second, last)
    onward = ((z + 1) % 4, (z + 3) % 4, (3 * z + 1) % 4)
    events = [(k, w) for k in range(3) for w in range(4)]
    forwards, stage1, stage2, stage3 = {}, {}, {}, {}

    def arrive(k, w):
        r, c = SHARES[w]
        o = origins[k]
        mine = outs[w].at[o, rows(quarter, r), cols(core, c)]
        forward = push(mine, mine, fs.at[w, k], zr.at[w, o], {"fsdp": onward[k]})
        forwards[k, w] = forward
        forward.wait_recv()
        pl.when(inner)(forward.start)
        step = 2 if BIT1_FIRST[w] else 4
        copy = push(mine, mine, s1.at[w, k], r1.at[w, k], {"seq": partner(me, step)})
        copy.start()
        stage1[k, w] = copy

    def pair(k, w):
        r, c = SHARES[w]
        o = origins[k]
        stage1[k, w].wait_recv()
        half = cols(core, c)
        if BIT1_FIRST[w]:
            blocks = [outs[w].at[o, rows(2 * b2, r, 2), half]]
            step = 4
        else:
            blocks = [outs[w].at[o, rows(b1 + 2 * j, r), half] for j in range(2)]
            step = 2
        stage2[k, w] = []
        for j, block in enumerate(blocks):
            copy = push(block, block, s2.at[w, k, j], r2.at[w, k, j], {"seq": partner(me, step)})
            copy.start()
            stage2[k, w].append(copy)

    def across(k, w):
        r, c = SHARES[w]
        for copy in stage2[k, w]:
            copy.wait_recv()
        block = outs[w].at[origins[k], :, cols(core, c)]
        copy = push(block, block, s3.at[w, k], r3.at[w, k], {"seq": partner(me, 1)})
        copy.start()
        stage3[k, w] = copy

    acts = (arrive, pair, across)
    for act, k, w in gather_order():
        acts[act](k, w)
    for event in events:
        stage3[event].wait_recv()
    for copy in copies:
        copy.wait()
    for up, down in own:
        pl.when(z < 3)(up.wait_send)
        pl.when(z > 0)(down.wait_send)
    for event in events:
        pl.when(inner)(forwards[event].wait_send)
        stage1[event].wait_send()
        for copy in stage2[event]:
            copy.wait_send()
        stage3[event].wait_send()


def gather_weights(shards):
    sem = pltpu.SemaphoreType.DMA
    return pl.pallas_call(
        gather_kernel,
        out_shape=[jax.ShapeDtypeStruct((4, 4 * r, 2 * c), jnp.bfloat16) for r, c in SHARES],
        in_specs=[pl.BlockSpec(memory_space=pltpu.VMEM)] * 4,
        out_specs=[pl.BlockSpec(memory_space=pl.ANY)] * 4,
        scratch_shapes=[
            sem((4,)), sem((4, 2)), sem((4, 4)), sem((4, 3)), sem((4, 3)), sem((4, 3)),
            sem((4, 3, 2)), sem((4, 3, 2)), sem((4, 3)), sem((4, 3)),
        ],
        compiler_params=pltpu.CompilerParams(
            collective_id=0, has_side_effects=True, vmem_limit_bytes=32 * 1024 * 1024
        ),
    )(*shards)


WIDE = 384
CHUNKS = ((2, 0), (2, 384), (2, 768), (1, 0), (0, 0), (0, 384), (0, 768), (3, 0))


def reduce_order():
    order = []
    for t in range(4 + 6):
        for act, lag in (
            ("finish", 6), ("across", 5), ("spread", 4), ("owner", 3), ("share", 2), ("pair", 0)
        ):
            if 0 <= t - lag < 4:
                order.append((act, t - lag))
    return order


def reduce_kernel(*refs):
    xin, yin, gin = refs[:4], (None,) + refs[4:7], refs[7]
    q, above, own, below, pos, grad, lse, cosine, sine, w_qkv, unit = refs[8:19]
    outs, dh_out = refs[19:24], refs[24]
    xb, yb, gb = refs[25:29], refs[29:33], refs[33]
    cs, b1s, s1s, b2s, s2s, bz, ag = (refs[34 + 8 * i : 42 + 8 * i] for i in range(7))
    csem, sem1, sem2, zsem, asem, hsem = refs[90:96]
    dq, up, mid, down, back_above, back_below, mixed, gsum, gmine = refs[96:]
    me, z, core, b1, b2 = place()
    quarter = b1 + 2 * b2
    after, before = (me + 1) % 8, (me + 7) % 8
    greet(me, z, (after, before))
    f32, low = jnp.float32, jnp.bfloat16
    sent = []
    table = {}

    def go(key, src, dst, sems, target):
        copy = push(src, dst, sems.at[0], sems.at[1], target)
        copy.start()
        sent.append(copy)
        table.setdefault(key, []).append(copy)

    def take(key):
        for copy in table[key]:
            copy.wait_recv()

    twin = {"seq": partner(me, 1)}
    lanes = cols(core, 128)
    for w in (2, 1, 3, 0):
        c = SHARES[w][1]
        go(("x", w), xin[w], xb[w].at[:, lanes], csem.at[0, w], twin)
        if w > 0:
            src = yin[w].at[:, cols(1 - core, c)]
            go(("x", w), src, yb[w].at[rows(core, 128)], csem.at[1, w], twin)
    for w in (2, 1, 3, 0):
        xb[w][:, lanes] = xin[w][...]
        if w > 0:
            yb[w][rows(core, 128), :] = yin[w][:, cols(core, SHARES[w][1])]

    def product(i):
        w, start = CHUNKS[i]
        height = 4 * SHARES[w][0]
        if start == 0:
            take(("x", w))

        def body(o, carry):
            left = xb[w][pl.ds(pl.multiple_of(o * height, 16), height), :]
            right = yb[w][:, start : start + WIDE]
            cs[i][o] = jnp.dot(left, right, preferred_element_type=f32).astype(low)
            return carry

        lax.fori_loop(0, 4, body, 0)

    def first(i):
        w = CHUNKS[i][0]
        r = SHARES[w][0]
        if BIT1_FIRST[w]:
            src = cs[i].at[:, rows(2 * (1 - b2), r, 2), :]
            go((1, i), src, b1s[i], sem1.at[i, 0], {"seq": partner(me, 4)})
        else:
            for j in range(2):
                src = cs[i].at[:, rows(1 - b1 + 2 * j, r), :]
                dst = b1s[i].at[:, pl.ds(j * r, r), :]
                go((1, i), src, dst, sem1.at[i, j], {"seq": partner(me, 2)})

    def pair(i):
        w = CHUNKS[i][0]
        r = SHARES[w][0]
        take((1, i))

        def body(t, carry):
            o, j = t // 2, t % 2
            block = 2 * b2 + j if BIT1_FIRST[w] else b1 + 2 * j
            there = pl.ds(pl.multiple_of(j * r, 16), r)
            mine = cs[i][o, rows(block, r), :].astype(f32)
            s1s[i][o, there, :] = (mine + b1s[i][o, there, :].astype(f32)).astype(low)
            return carry

        lax.fori_loop(0, 8, body, 0)
        bit, step = (b1, 2) if BIT1_FIRST[w] else (b2, 4)
        src = s1s[i].at[:, rows(1 - bit, r), :]
        go((2, i), src, b2s[i], sem2.at[i], {"seq": partner(me, step)})

    def share(i):
        w = CHUNKS[i][0]
        r = SHARES[w][0]
        take((2, i))
        bit = b1 if BIT1_FIRST[w] else b2

        def body(o, carry):
            mine = s1s[i][o, rows(bit, r), :].astype(f32)
            s2s[i][o] = (mine + b2s[i][o].astype(f32)).astype(low)
            return carry

        lax.fori_loop(0, 4, body, 0)
        for d in (2, 1, 3):
            to = (z + d) % 4
            go((3, i), s2s[i].at[to], bz[i].at[d - 1], zsem.at[i, d - 1], {"fsdp": to})

    def owner(i):
        w = CHUNKS[i][0]
        r = SHARES[w][0]
        take((3, i))
        total = s2s[i][z].astype(f32)
        for d in range(3):
            total = total + bz[i][d].astype(f32)
        ag[i][core, rows(quarter, r), :] = total.astype(low)
        block = ag[i].at[core, rows(quarter, r), :]
        step = 2 if BIT1_FIRST[w] else 4
        go((4, i), block, block, asem.at[i, 0], {"seq": partner(me, step)})

    def spread(i):
        w = CHUNKS[i][0]
        r = SHARES[w][0]
        take((4, i))
        if BIT1_FIRST[w]:
            block = ag[i].at[core, rows(2 * b2, r, 2), :]
            go((5, i), block, block, asem.at[i, 1], {"seq": partner(me, 4)})
        else:
            for j in range(2):
                block = ag[i].at[core, rows(b1 + 2 * j, r), :]
                go((5, i), block, block, asem.at[i, 1 + j], {"seq": partner(me, 2)})

    def across(i):
        take((5, i))
        block = ag[i].at[core]
        go((6, i), block, block, asem.at[i, 3], twin)

    def finish(i):
        w, start = CHUNKS[i]
        r, c = SHARES[w]
        take((6, i))

        def body(t, carry):
            part = pl.ds(pl.multiple_of(t * r, 16), r)
            for half in range(2):
                at = half * c + start
                outs[w][part, at : at + WIDE] = ag[i][half, part, :].astype(f32)
            return carry

        if w < 3:
            lax.fori_loop(0, 4, body, 0)
            return
        lax.fori_loop(0, 3, body, 0)
        for half in range(2):
            at = half * c
            for to, begin, end in ((3, 3 * r, 4 * r - PAD), (4, 4 * r - PAD, 4 * r)):
                low_row = begin if to == 3 else 0
                part = ag[i][half, begin:end, :].astype(f32)
                outs[to][low_row : low_row + end - begin, at : at + WIDE] = part

    acts = {
        "first": first, "pair": pair, "share": share, "owner": owner,
        "spread": spread, "across": across, "finish": finish,
    }
    for i in range(4):
        product(i)
        first(i)
    product(7)
    attend_back_kernel(
        q, above, own, below, pos, grad, lse, cosine, sine, dq, up, mid, down
    )
    to_before = push(up, back_below, hsem.at[0, 0], hsem.at[0, 1], {"seq": before})
    to_after = push(down, back_above, hsem.at[1, 0], hsem.at[1, 1], {"seq": after})
    pl.when(me > 0)(to_before.start)
    pl.when(me < 7)(to_after.start)

    @pl.when(me == 0)
    def _():
        back_above[...] = jnp.zeros_like(back_above)

    @pl.when(me == 7)
    def _():
        back_below[...] = jnp.zeros_like(back_below)

    pl.when(me > 0)(to_after.wait_recv)
    pl.when(me < 7)(to_before.wait_recv)
    join_kernel(dq, mid, back_above, back_below, cosine, sine, mixed)
    c = SHARES[0][1]
    go(("x", 0), mixed.at[:, cols(1 - core, c)], yb[0].at[rows(core, 128)], csem.at[1, 0], twin)
    yb[0][rows(core, 128), :] = mixed[:, cols(core, c)]
    for i in (4, 5, 6):
        product(i)
        first(i)
    for g in range(D // 128):
        at = slice(128 * g, 128 * g + 128)
        dh = dot_rows(mixed[...], w_qkv[at, :])
        dh_out[:, at] = dh
        gsum[0:1, at] = jnp.sum(dh * unit[:, at], axis=0, keepdims=True)
    held = D // 4
    for o in range(4):
        piece = gsum[0:1, held * o : held * o + held]
        piece = jnp.concatenate([piece, jnp.zeros((1, D - held), f32)], axis=1)
        gmine[o] = (gin[o].astype(f32) + jnp.broadcast_to(piece, (PAD, D))).astype(low)
    go("g", gmine.at[:, :, cols(1 - core, WIDE)], gb, csem.at[2, 0], twin)
    take("g")
    kept = gmine[:, :, cols(core, WIDE)].astype(f32)
    cs[7][:, 4 * SHARES[3][0] - PAD :, :] = (kept + gb[...].astype(f32)).astype(low)
    first(7)
    for act, p in reduce_order():
        for i in (2 * p, 2 * p + 1):
            acts[act](i)
    for copy in sent:
        copy.wait_send()
    pl.when(me > 0)(to_before.wait_send)
    pl.when(me < 7)(to_after.wait_send)


def reduce_grads(lefts, rights, gain_rows, attention):
    sem = pltpu.SemaphoreType.DMA
    vmem = lambda *shape: pltpu.VMEM(shape, jnp.bfloat16)
    heights = [SHARES[w][0] for w, start in CHUNKS]
    count = len(CHUNKS)
    shapes = [(4 * r, 2 * c) for r, c in SHARES]
    shapes = shapes[:3] + [(shapes[3][0] - PAD, shapes[3][1]), (PAD, shapes[3][1]), (128, D)]
    rim = (HALF_WINDOW, 2 * D)
    return pl.pallas_call(
        reduce_kernel,
        out_shape=[jax.ShapeDtypeStruct(shape, jnp.float32) for shape in shapes],
        in_specs=[pl.BlockSpec(memory_space=pltpu.VMEM)] * 19,
        out_specs=[pl.BlockSpec(memory_space=pltpu.VMEM)] * 6,
        scratch_shapes=[vmem(16 * r, 256) for r, c in SHARES]
        + [vmem(256, c) for r, c in SHARES]
        + [vmem(4, PAD, WIDE)]
        + [vmem(4, 4 * r, WIDE) for r in heights]
        + [vmem(4, 2 * r, WIDE) for r in heights] * 2
        + [vmem(4, r, WIDE) for r in heights] * 2
        + [vmem(3, r, WIDE) for r in heights]
        + [vmem(2, 4 * r, WIDE) for r in heights]
        + [
            sem((3, 4, 2)), sem((count, 2, 2)), sem((count, 2)), sem((count, 3, 2)),
            sem((count, 4, 2)), sem((2, 2)),
        ]
        + [vmem(128, D), vmem(*rim), pltpu.VMEM((128, 2 * D), jnp.float32)]
        + [vmem(*rim), vmem(*rim), vmem(*rim), vmem(128, 3 * D)]
        + [pltpu.VMEM((8, D), jnp.float32), vmem(4, PAD, D)],
        compiler_params=pltpu.CompilerParams(
            collective_id=1, has_side_effects=True, vmem_limit_bytes=56 * 1024 * 1024
        ),
    )(*lefts, *rights, gain_rows, *attention)


def swap_halves(values):
    lane = lax.broadcasted_iota(jnp.int32, values.shape, 1)
    return jnp.where(lane % 64 < 32, pltpu.roll(values, 96, 1), pltpu.roll(values, 32, 1))


def turn_kernel(mixed, cosine, sine, flags, q_out, kv_out):
    cos, sin = cosine[...], sine[...]
    for g in range(2 * D // 128):
        u = mixed[:, 128 * g : 128 * g + 128]
        turned = (u * cos + swap_halves(u) * sin).astype(jnp.bfloat16)
        if g < D // 128:
            q_out[:, 128 * g : 128 * g + 128] = turned
        else:
            at = 128 * g - D
            kv_out[:, at : at + 128] = turned
    kv_out[:, D : 2 * D] = mixed[:, 2 * D :].astype(jnp.bfloat16)
    kv_out[:, 2 * D :] = jnp.broadcast_to(flags[...], (flags.shape[0], 128)).astype(jnp.bfloat16)


def widen(above, own, below, start, size):
    return jnp.concatenate([ref[:, start : start + size] for ref in (above, own, below)], axis=0)


def visible(above, own, below, pos):
    flag = widen(above, own, below, 2 * D, 128).astype(jnp.float32).T
    shape = flag.shape
    offset = (
        lax.broadcasted_iota(jnp.int32, shape, 1)
        - HALF_WINDOW
        - lax.broadcasted_iota(jnp.int32, shape, 0)
    ).astype(jnp.float32)
    place_of = jnp.broadcast_to(pos[...], shape)
    earlier = (offset >= 0.0) | (place_of >= -offset)
    later = (offset < 0.0) | (flag - 1.0 >= offset)
    return (jnp.abs(offset) <= HALF_WINDOW) & (flag > 0.5) & earlier & later


def dot_rows(left, right):
    return lax.dot_general(
        left, right, (((1,), (1,)), ((), ())), preferred_element_type=jnp.float32
    )


def attend_kernel(q, above, own, below, pos, o_out, lse_out):
    allowed = visible(above, own, below, pos)
    scale = HEAD_DIM ** (-0.5)
    lane = lax.broadcasted_iota(jnp.int32, lse_out.shape, 1)
    kept = jnp.zeros(lse_out.shape, jnp.float32)
    for g in range(HEADS // 2):
        keys = widen(above, own, below, 128 * g, 128)
        values = widen(above, own, below, D + 128 * g, 128)
        queries = q[:, 128 * g : 128 * g + 128]
        outs = []
        for j in range(2):
            part = slice(64 * j, 64 * j + 64)
            scores = dot_rows(queries[:, part], keys[:, part]) * scale
            scores = jnp.where(allowed, scores, masked_score)
            top = jnp.max(scores, axis=-1, keepdims=True)
            expo = jnp.exp(scores - top)
            total = jnp.sum(expo, axis=-1, keepdims=True)
            kept = jnp.where(lane == 2 * g + j, top + jnp.log(total), kept)
            probs = (expo / total).astype(jnp.bfloat16)
            outs.append(jnp.dot(probs, values[:, part], preferred_element_type=jnp.float32))
        o_out[:, 128 * g : 128 * g + 128] = jnp.concatenate(outs, axis=1).astype(jnp.bfloat16)
    lse_out[...] = kept


def attend_back_kernel(
    q, above, own, below, pos, grad, lse, cosine, sine, dq_out, up_out, mid_out, down_out
):
    allowed = visible(above, own, below, pos)
    scale = HEAD_DIM ** (-0.5)
    cos, sin = cosine[...], sine[...]
    low = jnp.bfloat16
    count = q.shape[0]
    edge = count + HALF_WINDOW
    for g in range(HEADS // 2):
        at = slice(128 * g, 128 * g + 128)
        keys = widen(above, own, below, 128 * g, 128)
        values = widen(above, own, below, D + 128 * g, 128)
        queries, grads = q[:, at], grad[:, at]
        dqs, dks, dvs = [], [], []
        for j in range(2):
            part = slice(64 * j, 64 * j + 64)
            head = 2 * g + j
            scores = dot_rows(queries[:, part], keys[:, part]) * scale
            scores = jnp.where(allowed, scores, masked_score)
            probs = jnp.exp(scores - lse[:, head : head + 1])
            probs_low = probs.astype(low)
            dp = dot_rows(grads[:, part], values[:, part])
            row = jnp.sum(probs * dp, axis=-1, keepdims=True)
            ds = (probs * (dp - row)).astype(low)
            dqs.append(jnp.dot(ds, keys[:, part], preferred_element_type=jnp.float32) * scale)
            dks.append(matmul_left(ds, queries[:, part]) * scale)
            dvs.append(matmul_left(probs_low, grads[:, part]))
        dq = jnp.concatenate(dqs, axis=1)
        dq_out[:, at] = (dq * cos - swap_halves(dq) * sin).astype(low)
        for start, pieces in ((0, dks), (D, dvs)):
            wide = jnp.concatenate(pieces, axis=1)
            to = slice(start + 128 * g, start + 128 * g + 128)
            up_out[:, to] = wide[:HALF_WINDOW].astype(low)
            mid_out[:, to] = wide[HALF_WINDOW:edge]
            down_out[:, to] = wide[edge:].astype(low)


def join_kernel(dq, mid, above, below, cosine, sine, out):
    cos, sin = cosine[...], sine[...]
    out[:, :D] = dq[...]
    for g in range(2 * D // 128):
        at = slice(128 * g, 128 * g + 128)
        back = jnp.concatenate([above[:, at], below[:, at]], axis=0).astype(jnp.float32)
        total = mid[:, at] + back
        if g < D // 128:
            total = total * cos - swap_halves(total) * sin
        out[:, D + 128 * g : D + 128 * g + 128] = total.astype(jnp.bfloat16)


def local_call(kernel, shapes, *operands):
    vmem = pl.BlockSpec(memory_space=pltpu.VMEM)
    return pl.pallas_call(
        kernel,
        out_shape=[jax.ShapeDtypeStruct(shape, kind) for shape, kind in shapes],
        in_specs=[vmem] * len(operands),
        out_specs=[vmem] * len(shapes),
        compiler_params=pltpu.CompilerParams(vmem_limit_bytes=32 * 1024 * 1024),
    )(*operands)


def neighbours(up, down):
    lanes = lax.axis_size("seq")
    above = lax.ppermute(down, "seq", [(i, i + 1) for i in range(lanes - 1)])
    below = lax.ppermute(up, "seq", [(i + 1, i) for i in range(lanes - 1)])
    return above, below


def on_device(inputs, positions, cotangent, w_qkv, w_out, w_in, w_down, gain_attn, gain_mlp):
    gains = jnp.concatenate([gain_attn, gain_mlp])
    gains = jnp.pad(gains[None], ((0, PAD - 1), (0, D - gains.shape[0])))
    packed = jnp.concatenate([w_down, gains], axis=0)
    full_qkv, full_out, full_in, full_packed = gather_weights([w_qkv, w_out, w_in, packed])
    full_qkv = full_qkv.reshape(D, 3 * D)
    full_out = full_out.reshape(D, D)
    full_in = full_in.reshape(D, 2 * FF)
    owned_rows = w_down.shape[0]
    full_down = full_packed[:, :owned_rows].reshape(FF, D)
    held = gain_attn.shape[0]
    gain_first = full_packed[:, owned_rows, :held].reshape(D).astype(jnp.float32)
    gain_second = full_packed[:, owned_rows, held : 2 * held].reshape(D).astype(jnp.float32)
    tokens = inputs[0].astype(jnp.float32)
    token_pos = positions[0]
    count = tokens.shape[0]
    normed, norm_back = jax.vjp(layer_norm, tokens, gain_first)
    normed_low = normed.astype(jnp.bfloat16)
    mixed = jnp.dot(normed_low, full_qkv, preferred_element_type=jnp.float32)
    half = HEAD_DIM // 2
    ladder = jnp.arange(half).astype(jnp.float32) * (2.0 / HEAD_DIM)
    angles = token_pos.astype(jnp.float32)[:, None] * (rope_base ** (-ladder))[None, :]
    cosine, sine = jnp.cos(angles), jnp.sin(angles)
    cosine = jnp.concatenate([cosine] * 4, axis=1)
    sine = jnp.concatenate([-sine, sine] * 2, axis=1)
    flags = (jnp.minimum(token_pos, 127) + 1).astype(jnp.float32)[:, None]
    pos = token_pos.astype(jnp.float32)[:, None]
    low = jnp.bfloat16
    query_low, key_value = local_call(
        turn_kernel, [((count, D), low), ((count, 2 * D + 128), low)], mixed, cosine, sine, flags
    )
    above, below = neighbours(key_value[:HALF_WINDOW], key_value[count - HALF_WINDOW :])
    attended_low, logsum = local_call(
        attend_kernel,
        [((count, D), low), ((count, 128), jnp.float32)],
        query_low, above, key_value, below, pos,
    )
    middle = tokens + jnp.dot(attended_low, full_out, preferred_element_type=jnp.float32)
    normed_mlp, mlp_norm_back = jax.vjp(layer_norm, middle, gain_second)
    normed_mlp_low = normed_mlp.astype(jnp.bfloat16)
    gate_up = jnp.dot(normed_mlp_low, full_in, preferred_element_type=jnp.float32)

    def geglu(paired):
        return jax.nn.gelu(paired[:, :FF], approximate=False) * paired[:, FF:]

    hidden, geglu_back = jax.vjp(geglu, gate_up)
    hidden_low = hidden.astype(jnp.bfloat16)
    result = middle + jnp.dot(hidden_low, full_down, preferred_element_type=jnp.float32)
    grad_result = cotangent[0]
    grad_down_local = matmul_left(hidden_low, grad_result)
    grad_hidden = matmul_right(grad_result, full_down)
    grad_gate_up = geglu_back(grad_hidden)[0].astype(jnp.bfloat16)
    grad_in_local = matmul_left(normed_mlp_low, grad_gate_up)
    grad_normed_mlp = matmul_right(grad_gate_up, full_in)
    grad_middle_norm, grad_gain_second = mlp_norm_back(grad_normed_mlp)
    grad_middle = grad_result.astype(jnp.float32) + grad_middle_norm
    grad_branch = grad_middle.astype(jnp.bfloat16)
    grad_out_local = matmul_left(attended_low, grad_branch)
    grad_attended = matmul_right(grad_branch, full_out).astype(low)
    lanes = lax.axis_size("seq")
    if lanes == 8:
        gain_rows = jnp.pad(
            grad_gain_second.reshape(4, 1, held),
            ((0, 0), (0, PAD - 1), (held, D - 2 * held)),
        )
        hidden_rows = jnp.pad(
            hidden_low.T.reshape(4, owned_rows, count), ((0, 0), (0, PAD), (0, 0))
        )
        grad_qkv, grad_out, grad_in, grad_down, gain_sums, grad_normed = reduce_grads(
            [normed_low.T, attended_low.T, normed_mlp_low.T, hidden_rows.reshape(-1, count)],
            [grad_branch, grad_gate_up, grad_result],
            gain_rows.astype(jnp.bfloat16),
            [
                query_low, above, key_value, below, pos, grad_attended, logsum, cosine, sine,
                full_qkv, layer_norm(tokens, jnp.ones_like(gain_first)),
            ],
        )
        grad_tokens = grad_middle + norm_back(grad_normed)[0]
        return (
            result[None].astype(jnp.bfloat16),
            grad_tokens[None],
            grad_qkv,
            grad_out,
            grad_in,
            grad_down,
            gain_sums[0, :held],
            gain_sums[0, held : 2 * held],
        )
    grad_query, up, own, down = local_call(
        attend_back_kernel,
        [
            ((count, D), low),
            ((HALF_WINDOW, 2 * D), low),
            ((count, 2 * D), jnp.float32),
            ((HALF_WINDOW, 2 * D), low),
        ],
        query_low, above, key_value, below, pos, grad_attended, logsum, cosine, sine,
    )
    back_above, back_below = neighbours(up, down)
    (grad_mixed,) = local_call(
        join_kernel, [((count, 3 * D), low)], grad_query, own, back_above, back_below, cosine, sine
    )
    grad_qkv_local = matmul_left(normed_low, grad_mixed)
    grad_normed = matmul_right(grad_mixed, full_qkv)
    grad_tokens_norm, grad_gain_first = norm_back(grad_normed)
    grad_tokens = grad_middle + grad_tokens_norm
    owned = (
        lax.psum_scatter(
            grad_qkv_local.astype(jnp.bfloat16), "fsdp", scatter_dimension=0, tiled=True
        ).astype(jnp.float32),
        lax.psum_scatter(
            grad_out_local.astype(jnp.bfloat16), "fsdp", scatter_dimension=0, tiled=True
        ).astype(jnp.float32),
        lax.psum_scatter(
            grad_in_local.astype(jnp.bfloat16), "fsdp", scatter_dimension=0, tiled=True
        ).astype(jnp.float32),
        lax.psum_scatter(
            grad_down_local.astype(jnp.bfloat16), "fsdp", scatter_dimension=0, tiled=True
        ).astype(jnp.float32),
        lax.psum_scatter(
            grad_gain_first.astype(jnp.bfloat16), "fsdp", scatter_dimension=0, tiled=True
        ).astype(jnp.float32),
        lax.psum_scatter(
            grad_gain_second.astype(jnp.bfloat16), "fsdp", scatter_dimension=0, tiled=True
        ).astype(jnp.float32),
    )
    owned_flat = pack_rows(owned, 1)
    owned_share = owned_flat.shape[1] // lanes
    lane_part = lax.psum_scatter(
        owned_flat.reshape(lanes, owned_share), "seq", scatter_dimension=0, tiled=True
    )
    summed_row = (
        lax.all_gather(lane_part.astype(jnp.bfloat16), "seq", axis=0, tiled=True)
        .astype(lane_part.dtype)
        .reshape(-1)
    )
    grad_qkv, grad_out, grad_in, grad_down, grad_gain_attn, grad_gain_mlp = unpack_row(
        summed_row, owned, 1
    )
    return (
        result[None].astype(jnp.bfloat16),
        grad_tokens[None],
        grad_qkv,
        grad_out,
        grad_in,
        grad_down,
        grad_gain_attn,
        grad_gain_mlp,
    )


def solution(mesh):
    in_specs = (
        P("fsdp", "seq", None),
        P("fsdp", "seq"),
        P("fsdp", "seq", None),
        P("fsdp", None),
        P("fsdp", None),
        P("fsdp", None),
        P("fsdp", None),
        P("fsdp"),
        P("fsdp"),
    )
    out_specs = (
        P("fsdp", "seq", None),
        P("fsdp", "seq", None),
        P("fsdp", None),
        P("fsdp", None),
        P("fsdp", None),
        P("fsdp", None),
        P("fsdp"),
        P("fsdp"),
    )
    return jax.shard_map(
        on_device, mesh=mesh, in_specs=in_specs, out_specs=out_specs, check_vma=False
    )
```

```python
import functools
import math

import jax
import jax.numpy as jnp
from jax import lax
from jax.experimental import pallas as pl
from jax.experimental.pallas import tpu as pltpu
from jax.sharding import PartitionSpec as P

D = 768
HEADS = 12
HEAD_DIM = 64
FF = 1152
HALF_WINDOW = 64


eps = 1e-05
rope_base = 10000.0
masked_score = -1e30


def layer_norm(values, gain):
    center = values - jnp.mean(values, axis=-1, keepdims=True)
    spread = jnp.mean(center * center, axis=-1, keepdims=True)
    return center * lax.rsqrt(spread + eps) * gain


def matmul_left(left, right):
    return lax.dot_general(
        left, right, (((0,), (0,)), ((), ())), preferred_element_type=jnp.float32
    )


def matmul_right(left, right):
    return lax.dot_general(
        left, right, (((1,), (1,)), ((), ())), preferred_element_type=jnp.float32
    )


def pack_rows(pieces, groups):
    joined = jnp.concatenate([piece.reshape(groups, -1) for piece in pieces], axis=1)
    return joined


def unpack_row(flat_row, pieces, groups):
    results = []
    offset = 0
    for piece in pieces:
        shape = (piece.shape[0] // groups,) + piece.shape[1:]
        size = math.prod(shape)
        results.append(flat_row[offset : offset + size].reshape(shape))
        offset = offset + size
    return results


MESH = pl.DeviceIdType.MESH
PAD = 32
SHARES = ((48, 1152), (48, 384), (48, 1152), (80, 384))
BIT1_FIRST = (True, True, False, False)


def partner(me, step):
    return me + step * (1 - 2 * ((me // step) % 2))


def place():
    me, z = lax.axis_index("seq"), lax.axis_index("fsdp")
    core, b1, b2 = me % 2, (me // 2) % 2, (me // 4) % 2
    return me, z, core, b1, b2


def greet(me, z, others=()):
    barrier = pltpu.get_barrier_semaphore()
    for other in others:
        pl.semaphore_signal(barrier, inc=1, device_id={"seq": other}, device_id_type=MESH)
    for step in (1, 2, 4):
        pl.semaphore_signal(
            barrier, inc=1, device_id={"seq": partner(me, step)}, device_id_type=MESH
        )
    for step in (1, 2, 3):
        pl.semaphore_signal(
            barrier, inc=1, device_id={"fsdp": (z + step) % 4}, device_id_type=MESH
        )
    pl.semaphore_wait(barrier, 6 + len(others))


def rows(block, size, count=1):
    return pl.ds(pl.multiple_of(block * size, 16), size * count)


def cols(half, size):
    return pl.ds(pl.multiple_of(half * size, 128), size)


def push(src, dst, send, recv, target):
    return pltpu.make_async_remote_copy(
        src_ref=src, dst_ref=dst, send_sem=send, recv_sem=recv,
        device_id=target, device_id_type=MESH,
    )


def gather_order():
    order = []
    for k in range(4):
        if k < 3:
            order += [(0, k, w) for w in range(4)]
        if k > 0:
            order += [(2, k - 1, w) for w in range(4)]
        if k < 3:
            order += [(1, k, w) for w in range(4)]
    return order


def gather_kernel(*refs):
    ins, outs = refs[:4], refs[4:8]
    local, zs, zr, fs, s1, r1, s2, r2, s3, r3 = refs[8:]
    me, z, core, b1, b2 = place()
    quarter = b1 + 2 * b2
    greet(me, z)
    inner = (z == 1) | (z == 2)
    sent = []
    own = []
    for w, (r, c) in enumerate(SHARES):
        src = ins[w].at[rows(quarter, r), cols(core, c)]
        dst = outs[w].at[z, rows(quarter, r), cols(core, c)]
        up = push(src, dst, zs.at[w, 0], zr.at[w, z], {"fsdp": lax.rem(z + 1, 4)})
        down = push(src, dst, zs.at[w, 1], zr.at[w, z], {"fsdp": lax.rem(z + 3, 4)})
        own.append((up, down))
        pl.when(z < 3)(up.start)
        pl.when(z > 0)(down.start)
    copies = []
    for w in range(4):
        copy = pltpu.make_async_copy(ins[w], outs[w].at[z], local.at[w])
        copy.start()
        copies.append(copy)
    first = (z + 3) % 4 - 2 * ((3 - z) // 3)
    last = 3 * (1 - z // 2)
    second = 6 - z - first - last
    origins = (first, second, last)
    onward = ((z + 1) % 4, (z + 3) % 4, (3 * z + 1) % 4)
    events = [(k, w) for k in range(3) for w in range(4)]
    forwards, stage1, stage2, stage3 = {}, {}, {}, {}

    def arrive(k, w):
        r, c = SHARES[w]
        o = origins[k]
        mine = outs[w].at[o, rows(quarter, r), cols(core, c)]
        forward = push(mine, mine, fs.at[w, k], zr.at[w, o], {"fsdp": onward[k]})
        forwards[k, w] = forward
        forward.wait_recv()
        pl.when(inner)(forward.start)
        step = 2 if BIT1_FIRST[w] else 4
        copy = push(mine, mine, s1.at[w, k], r1.at[w, k], {"seq": partner(me, step)})
        copy.start()
        stage1[k, w] = copy

    def pair(k, w):
        r, c = SHARES[w]
        o = origins[k]
        stage1[k, w].wait_recv()
        half = cols(core, c)
        if BIT1_FIRST[w]:
            blocks = [outs[w].at[o, rows(2 * b2, r, 2), half]]
            step = 4
        else:
            blocks = [outs[w].at[o, rows(b1 + 2 * j, r), half] for j in range(2)]
            step = 2
        stage2[k, w] = []
        for j, block in enumerate(blocks):
            copy = push(block, block, s2.at[w, k, j], r2.at[w, k, j], {"seq": partner(me, step)})
            copy.start()
            stage2[k, w].append(copy)

    def across(k, w):
        r, c = SHARES[w]
        for copy in stage2[k, w]:
            copy.wait_recv()
        block = outs[w].at[origins[k], :, cols(core, c)]
        copy = push(block, block, s3.at[w, k], r3.at[w, k], {"seq": partner(me, 1)})
        copy.start()
        stage3[k, w] = copy

    acts = (arrive, pair, across)
    for act, k, w in gather_order():
        acts[act](k, w)
    for event in events:
        stage3[event].wait_recv()
    for copy in copies:
        copy.wait()
    for up, down in own:
        pl.when(z < 3)(up.wait_send)
        pl.when(z > 0)(down.wait_send)
    for event in events:
        pl.when(inner)(forwards[event].wait_send)
        stage1[event].wait_send()
        for copy in stage2[event]:
            copy.wait_send()
        stage3[event].wait_send()


def gather_weights(shards):
    sem = pltpu.SemaphoreType.DMA
    return pl.pallas_call(
        gather_kernel,
        out_shape=[jax.ShapeDtypeStruct((4, 4 * r, 2 * c), jnp.bfloat16) for r, c in SHARES],
        in_specs=[pl.BlockSpec(memory_space=pltpu.VMEM)] * 4,
        out_specs=[pl.BlockSpec(memory_space=pl.ANY)] * 4,
        scratch_shapes=[
            sem((4,)), sem((4, 2)), sem((4, 4)), sem((4, 3)), sem((4, 3)), sem((4, 3)),
            sem((4, 3, 2)), sem((4, 3, 2)), sem((4, 3)), sem((4, 3)),
        ],
        compiler_params=pltpu.CompilerParams(
            collective_id=0, has_side_effects=True, vmem_limit_bytes=32 * 1024 * 1024
        ),
    )(*shards)


WIDE = 384
CHUNKS = ((2, 0), (2, 384), (2, 768), (1, 0), (0, 0), (0, 384), (0, 768), (3, 0))


CHUNK_BIT1 = (False, False, True, True, False, True, True, False)


def reduce_order():
    early, late = range(4), range(4, 8)
    order = []
    for i in early:
        order += [("owner", i), ("pair", 4 + i)]
    for i in early:
        order += [("spread", i), ("share", 4 + i)]
    for i in early:
        order += [("across", i), ("owner", 4 + i)]
    order += [("spread", i) for i in late]
    order += [("finish", i) for i in early]
    for act in ("across", "finish"):
        order += [(act, i) for i in late]
    return order


def reduce_kernel(*refs):
    xin, yin, gin = refs[:4], (None,) + refs[4:7], refs[7]
    q, above, own, below, pos, grad, lse, cosine, sine, w_qkv, unit = refs[8:19]
    outs, dh_out = refs[19:24], refs[24]
    xb, yb, gb = refs[25:29], refs[29:33], refs[33]
    cs, b1s, s1s, b2s, s2s, bz, ag = (refs[34 + 8 * i : 42 + 8 * i] for i in range(7))
    csem, sem1, sem2, zsem, asem, hsem = refs[90:96]
    dq, up, mid, down, back_above, back_below, mixed, gsum, gmine = refs[96:]
    me, z, core, b1, b2 = place()
    quarter = b1 + 2 * b2
    after, before = (me + 1) % 8, (me + 7) % 8
    greet(me, z, (after, before))
    f32, low = jnp.float32, jnp.bfloat16
    sent = []
    table = {}

    def go(key, src, dst, sems, target):
        copy = push(src, dst, sems.at[0], sems.at[1], target)
        copy.start()
        sent.append(copy)
        table.setdefault(key, []).append(copy)

    def take(key):
        for copy in table[key]:
            copy.wait_recv()

    twin = {"seq": partner(me, 1)}
    lanes = cols(core, 128)
    for w in (2, 1, 3, 0):
        c = SHARES[w][1]
        go(("x", w), xin[w], xb[w].at[:, lanes], csem.at[0, w], twin)
        if w > 0:
            src = yin[w].at[:, cols(1 - core, c)]
            go(("x", w), src, yb[w].at[rows(core, 128)], csem.at[1, w], twin)
    for w in (2, 1, 3, 0):
        xb[w][:, lanes] = xin[w][...]
        if w > 0:
            yb[w][rows(core, 128), :] = yin[w][:, cols(core, SHARES[w][1])]

    def product(i):
        w, start = CHUNKS[i]
        height = 4 * SHARES[w][0]
        if start == 0:
            take(("x", w))

        def body(o, carry):
            left = xb[w][pl.ds(pl.multiple_of(o * height, 16), height), :]
            right = yb[w][:, start : start + WIDE]
            cs[i][o] = jnp.dot(left, right, preferred_element_type=f32).astype(low)
            return carry

        lax.fori_loop(0, 4, body, 0)

    def first(i):
        w = CHUNKS[i][0]
        r = SHARES[w][0]
        if CHUNK_BIT1[i]:
            src = cs[i].at[:, rows(2 * (1 - b2), r, 2), :]
            go((1, i), src, b1s[i], sem1.at[i, 0], {"seq": partner(me, 4)})
        else:
            for j in range(2):
                src = cs[i].at[:, rows(1 - b1 + 2 * j, r), :]
                dst = b1s[i].at[:, pl.ds(j * r, r), :]
                go((1, i), src, dst, sem1.at[i, j], {"seq": partner(me, 2)})

    def pair(i):
        w = CHUNKS[i][0]
        r = SHARES[w][0]
        take((1, i))

        def body(t, carry):
            o, j = t // 2, t % 2
            block = 2 * b2 + j if CHUNK_BIT1[i] else b1 + 2 * j
            there = pl.ds(pl.multiple_of(j * r, 16), r)
            mine = cs[i][o, rows(block, r), :].astype(f32)
            s1s[i][o, there, :] = (mine + b1s[i][o, there, :].astype(f32)).astype(low)
            return carry

        lax.fori_loop(0, 8, body, 0)
        bit, step = (b1, 2) if CHUNK_BIT1[i] else (b2, 4)
        src = s1s[i].at[:, rows(1 - bit, r), :]
        go((2, i), src, b2s[i], sem2.at[i], {"seq": partner(me, step)})

    def share(i):
        w = CHUNKS[i][0]
        r = SHARES[w][0]
        take((2, i))
        bit = b1 if CHUNK_BIT1[i] else b2

        def body(o, carry):
            mine = s1s[i][o, rows(bit, r), :].astype(f32)
            s2s[i][o] = (mine + b2s[i][o].astype(f32)).astype(low)
            return carry

        lax.fori_loop(0, 4, body, 0)
        for d in (2, 1, 3):
            to = (z + d) % 4
            go((3, i), s2s[i].at[to], bz[i].at[d - 1], zsem.at[i, d - 1], {"fsdp": to})

    def owner(i):
        w = CHUNKS[i][0]
        r = SHARES[w][0]
        take((3, i))
        total = s2s[i][z].astype(f32)
        for d in range(3):
            total = total + bz[i][d].astype(f32)
        ag[i][core, rows(quarter, r), :] = total.astype(low)
        block = ag[i].at[core, rows(quarter, r), :]
        step = 2 if CHUNK_BIT1[i] else 4
        go((4, i), block, block, asem.at[i, 0], {"seq": partner(me, step)})

    def spread(i):
        w = CHUNKS[i][0]
        r = SHARES[w][0]
        take((4, i))
        if CHUNK_BIT1[i]:
            block = ag[i].at[core, rows(2 * b2, r, 2), :]
            go((5, i), block, block, asem.at[i, 1], {"seq": partner(me, 4)})
        else:
            for j in range(2):
                block = ag[i].at[core, rows(b1 + 2 * j, r), :]
                go((5, i), block, block, asem.at[i, 1 + j], {"seq": partner(me, 2)})

    def across(i):
        take((5, i))
        block = ag[i].at[core]
        go((6, i), block, block, asem.at[i, 3], twin)

    def finish(i):
        w, start = CHUNKS[i]
        r, c = SHARES[w]
        take((6, i))

        def body(t, carry):
            part = pl.ds(pl.multiple_of(t * r, 16), r)
            for half in range(2):
                at = half * c + start
                outs[w][part, at : at + WIDE] = ag[i][half, part, :].astype(f32)
            return carry

        if w < 3:
            lax.fori_loop(0, 4, body, 0)
            return
        lax.fori_loop(0, 3, body, 0)
        for half in range(2):
            at = half * c
            for to, begin, end in ((3, 3 * r, 4 * r - PAD), (4, 4 * r - PAD, 4 * r)):
                low_row = begin if to == 3 else 0
                part = ag[i][half, begin:end, :].astype(f32)
                outs[to][low_row : low_row + end - begin, at : at + WIDE] = part

    acts = {
        "first": first, "pair": pair, "share": share, "owner": owner,
        "spread": spread, "across": across, "finish": finish,
    }
    for i in range(4):
        product(i)
        first(i)
    product(7)
    attend_back_kernel(
        q, above, own, below, pos, grad, lse, cosine, sine, dq, up, mid, down
    )
    to_before = push(up, back_below, hsem.at[0, 0], hsem.at[0, 1], {"seq": before})
    to_after = push(down, back_above, hsem.at[1, 0], hsem.at[1, 1], {"seq": after})
    pl.when(me > 0)(to_before.start)
    pl.when(me < 7)(to_after.start)

    for i in range(4):
        pair(i)

    @pl.when(me == 0)
    def _():
        back_above[...] = jnp.zeros_like(back_above)

    @pl.when(me == 7)
    def _():
        back_below[...] = jnp.zeros_like(back_below)

    pl.when(me > 0)(to_after.wait_recv)
    pl.when(me < 7)(to_before.wait_recv)
    join_kernel(dq, mid, back_above, back_below, cosine, sine, mixed)
    c = SHARES[0][1]
    go(("x", 0), mixed.at[:, cols(1 - core, c)], yb[0].at[rows(core, 128)], csem.at[1, 0], twin)
    yb[0][rows(core, 128), :] = mixed[:, cols(core, c)]
    for i in (4, 5, 6):
        product(i)
        first(i)
    for i in range(4):
        share(i)
    for g in range(D // 128):
        at = slice(128 * g, 128 * g + 128)
        dh = dot_rows(mixed[...], w_qkv[at, :])
        dh_out[:, at] = dh
        gsum[0:1, at] = jnp.sum(dh * unit[:, at], axis=0, keepdims=True)
    held = D // 4
    for o in range(4):
        piece = gsum[0:1, held * o : held * o + held]
        piece = jnp.concatenate([piece, jnp.zeros((1, D - held), f32)], axis=1)
        gmine[o] = (gin[o].astype(f32) + jnp.broadcast_to(piece, (PAD, D))).astype(low)
    go("g", gmine.at[:, :, cols(1 - core, WIDE)], gb, csem.at[2, 0], twin)
    take("g")
    kept = gmine[:, :, cols(core, WIDE)].astype(f32)
    cs[7][:, 4 * SHARES[3][0] - PAD :, :] = (kept + gb[...].astype(f32)).astype(low)
    first(7)
    for act, i in reduce_order():
        acts[act](i)
    for copy in sent:
        copy.wait_send()
    pl.when(me > 0)(to_before.wait_send)
    pl.when(me < 7)(to_after.wait_send)


def reduce_grads(lefts, rights, gain_rows, attention):
    sem = pltpu.SemaphoreType.DMA
    vmem = lambda *shape: pltpu.VMEM(shape, jnp.bfloat16)
    heights = [SHARES[w][0] for w, start in CHUNKS]
    count = len(CHUNKS)
    shapes = [(4 * r, 2 * c) for r, c in SHARES]
    shapes = shapes[:3] + [(shapes[3][0] - PAD, shapes[3][1]), (PAD, shapes[3][1]), (128, D)]
    rim = (HALF_WINDOW, 2 * D)
    return pl.pallas_call(
        reduce_kernel,
        out_shape=[jax.ShapeDtypeStruct(shape, jnp.float32) for shape in shapes],
        in_specs=[pl.BlockSpec(memory_space=pltpu.VMEM)] * 19,
        out_specs=[pl.BlockSpec(memory_space=pltpu.VMEM)] * 6,
        scratch_shapes=[vmem(16 * r, 256) for r, c in SHARES]
        + [vmem(256, c) for r, c in SHARES]
        + [vmem(4, PAD, WIDE)]
        + [vmem(4, 4 * r, WIDE) for r in heights]
        + [vmem(4, 2 * r, WIDE) for r in heights] * 2
        + [vmem(4, r, WIDE) for r in heights] * 2
        + [vmem(3, r, WIDE) for r in heights]
        + [vmem(2, 4 * r, WIDE) for r in heights]
        + [
            sem((3, 4, 2)), sem((count, 2, 2)), sem((count, 2)), sem((count, 3, 2)),
            sem((count, 4, 2)), sem((2, 2)),
        ]
        + [vmem(128, D), vmem(*rim), pltpu.VMEM((128, 2 * D), jnp.float32)]
        + [vmem(*rim), vmem(*rim), vmem(*rim), vmem(128, 3 * D)]
        + [pltpu.VMEM((8, D), jnp.float32), vmem(4, PAD, D)],
        compiler_params=pltpu.CompilerParams(
            collective_id=1, has_side_effects=True, vmem_limit_bytes=56 * 1024 * 1024
        ),
    )(*lefts, *rights, gain_rows, *attention)


def swap_halves(values):
    lane = lax.broadcasted_iota(jnp.int32, values.shape, 1)
    return jnp.where(lane % 64 < 32, pltpu.roll(values, 96, 1), pltpu.roll(values, 32, 1))


def turn_kernel(mixed, cosine, sine, flags, q_out, kv_out):
    cos, sin = cosine[...], sine[...]
    for g in range(2 * D // 128):
        u = mixed[:, 128 * g : 128 * g + 128]
        turned = (u * cos + swap_halves(u) * sin).astype(jnp.bfloat16)
        if g < D // 128:
            q_out[:, 128 * g : 128 * g + 128] = turned
        else:
            at = 128 * g - D
            kv_out[:, at : at + 128] = turned
    kv_out[:, D : 2 * D] = mixed[:, 2 * D :].astype(jnp.bfloat16)
    kv_out[:, 2 * D :] = jnp.broadcast_to(flags[...], (flags.shape[0], 128)).astype(jnp.bfloat16)


def widen(above, own, below, start, size):
    return jnp.concatenate([ref[:, start : start + size] for ref in (above, own, below)], axis=0)


def visible(above, own, below, pos):
    flag = widen(above, own, below, 2 * D, 128).astype(jnp.float32).T
    shape = flag.shape
    offset = (
        lax.broadcasted_iota(jnp.int32, shape, 1)
        - HALF_WINDOW
        - lax.broadcasted_iota(jnp.int32, shape, 0)
    ).astype(jnp.float32)
    place_of = jnp.broadcast_to(pos[...], shape)
    earlier = (offset >= 0.0) | (place_of >= -offset)
    later = (offset < 0.0) | (flag - 1.0 >= offset)
    return (jnp.abs(offset) <= HALF_WINDOW) & (flag > 0.5) & earlier & later


def dot_rows(left, right):
    return lax.dot_general(
        left, right, (((1,), (1,)), ((), ())), preferred_element_type=jnp.float32
    )


def attend_kernel(q, above, own, below, pos, o_out, lse_out):
    allowed = visible(above, own, below, pos)
    scale = HEAD_DIM ** (-0.5)
    lane = lax.broadcasted_iota(jnp.int32, lse_out.shape, 1)
    kept = jnp.zeros(lse_out.shape, jnp.float32)
    for g in range(HEADS // 2):
        keys = widen(above, own, below, 128 * g, 128)
        values = widen(above, own, below, D + 128 * g, 128)
        queries = q[:, 128 * g : 128 * g + 128]
        outs = []
        for j in range(2):
            part = slice(64 * j, 64 * j + 64)
            scores = dot_rows(queries[:, part], keys[:, part]) * scale
            scores = jnp.where(allowed, scores, masked_score)
            top = jnp.max(scores, axis=-1, keepdims=True)
            expo = jnp.exp(scores - top)
            total = jnp.sum(expo, axis=-1, keepdims=True)
            kept = jnp.where(lane == 2 * g + j, top + jnp.log(total), kept)
            probs = (expo / total).astype(jnp.bfloat16)
            outs.append(jnp.dot(probs, values[:, part], preferred_element_type=jnp.float32))
        o_out[:, 128 * g : 128 * g + 128] = jnp.concatenate(outs, axis=1).astype(jnp.bfloat16)
    lse_out[...] = kept


def attend_back_kernel(
    q, above, own, below, pos, grad, lse, cosine, sine, dq_out, up_out, mid_out, down_out
):
    allowed = visible(above, own, below, pos)
    scale = HEAD_DIM ** (-0.5)
    cos, sin = cosine[...], sine[...]
    low = jnp.bfloat16
    count = q.shape[0]
    edge = count + HALF_WINDOW
    for g in range(HEADS // 2):
        at = slice(128 * g, 128 * g + 128)
        keys = widen(above, own, below, 128 * g, 128)
        values = widen(above, own, below, D + 128 * g, 128)
        queries, grads = q[:, at], grad[:, at]
        dqs, dks, dvs = [], [], []
        for j in range(2):
            part = slice(64 * j, 64 * j + 64)
            head = 2 * g + j
            scores = dot_rows(queries[:, part], keys[:, part]) * scale
            scores = jnp.where(allowed, scores, masked_score)
            probs = jnp.exp(scores - lse[:, head : head + 1])
            probs_low = probs.astype(low)
            dp = dot_rows(grads[:, part], values[:, part])
            row = jnp.sum(probs * dp, axis=-1, keepdims=True)
            ds = (probs * (dp - row)).astype(low)
            dqs.append(jnp.dot(ds, keys[:, part], preferred_element_type=jnp.float32) * scale)
            dks.append(matmul_left(ds, queries[:, part]) * scale)
            dvs.append(matmul_left(probs_low, grads[:, part]))
        dq = jnp.concatenate(dqs, axis=1)
        dq_out[:, at] = (dq * cos - swap_halves(dq) * sin).astype(low)
        for start, pieces in ((0, dks), (D, dvs)):
            wide = jnp.concatenate(pieces, axis=1)
            to = slice(start + 128 * g, start + 128 * g + 128)
            up_out[:, to] = wide[:HALF_WINDOW].astype(low)
            mid_out[:, to] = wide[HALF_WINDOW:edge]
            down_out[:, to] = wide[edge:].astype(low)


def join_kernel(dq, mid, above, below, cosine, sine, out):
    cos, sin = cosine[...], sine[...]
    out[:, :D] = dq[...]
    for g in range(2 * D // 128):
        at = slice(128 * g, 128 * g + 128)
        back = jnp.concatenate([above[:, at], below[:, at]], axis=0).astype(jnp.float32)
        total = mid[:, at] + back
        if g < D // 128:
            total = total * cos - swap_halves(total) * sin
        out[:, D + 128 * g : D + 128 * g + 128] = total.astype(jnp.bfloat16)


def local_call(kernel, shapes, *operands):
    vmem = pl.BlockSpec(memory_space=pltpu.VMEM)
    return pl.pallas_call(
        kernel,
        out_shape=[jax.ShapeDtypeStruct(shape, kind) for shape, kind in shapes],
        in_specs=[vmem] * len(operands),
        out_specs=[vmem] * len(shapes),
        compiler_params=pltpu.CompilerParams(vmem_limit_bytes=32 * 1024 * 1024),
    )(*operands)


def neighbours(up, down):
    lanes = lax.axis_size("seq")
    above = lax.ppermute(down, "seq", [(i, i + 1) for i in range(lanes - 1)])
    below = lax.ppermute(up, "seq", [(i + 1, i) for i in range(lanes - 1)])
    return above, below


def on_device(inputs, positions, cotangent, w_qkv, w_out, w_in, w_down, gain_attn, gain_mlp):
    gains = jnp.concatenate([gain_attn, gain_mlp])
    gains = jnp.pad(gains[None], ((0, PAD - 1), (0, D - gains.shape[0])))
    packed = jnp.concatenate([w_down, gains], axis=0)
    full_qkv, full_out, full_in, full_packed = gather_weights([w_qkv, w_out, w_in, packed])
    full_qkv = full_qkv.reshape(D, 3 * D)
    full_out = full_out.reshape(D, D)
    full_in = full_in.reshape(D, 2 * FF)
    owned_rows = w_down.shape[0]
    full_down = full_packed[:, :owned_rows].reshape(FF, D)
    held = gain_attn.shape[0]
    gain_first = full_packed[:, owned_rows, :held].reshape(D).astype(jnp.float32)
    gain_second = full_packed[:, owned_rows, held : 2 * held].reshape(D).astype(jnp.float32)
    tokens = inputs[0].astype(jnp.float32)
    token_pos = positions[0]
    count = tokens.shape[0]
    normed, norm_back = jax.vjp(layer_norm, tokens, gain_first)
    normed_low = normed.astype(jnp.bfloat16)
    mixed = jnp.dot(normed_low, full_qkv, preferred_element_type=jnp.float32)
    half = HEAD_DIM // 2
    ladder = jnp.arange(half).astype(jnp.float32) * (2.0 / HEAD_DIM)
    angles = token_pos.astype(jnp.float32)[:, None] * (rope_base ** (-ladder))[None, :]
    cosine, sine = jnp.cos(angles), jnp.sin(angles)
    cosine = jnp.concatenate([cosine] * 4, axis=1)
    sine = jnp.concatenate([-sine, sine] * 2, axis=1)
    flags = (jnp.minimum(token_pos, 127) + 1).astype(jnp.float32)[:, None]
    pos = token_pos.astype(jnp.float32)[:, None]
    low = jnp.bfloat16
    query_low, key_value = local_call(
        turn_kernel, [((count, D), low), ((count, 2 * D + 128), low)], mixed, cosine, sine, flags
    )
    above, below = neighbours(key_value[:HALF_WINDOW], key_value[count - HALF_WINDOW :])
    attended_low, logsum = local_call(
        attend_kernel,
        [((count, D), low), ((count, 128), jnp.float32)],
        query_low, above, key_value, below, pos,
    )
    middle = tokens + jnp.dot(attended_low, full_out, preferred_element_type=jnp.float32)
    normed_mlp, mlp_norm_back = jax.vjp(layer_norm, middle, gain_second)
    normed_mlp_low = normed_mlp.astype(jnp.bfloat16)
    gate_up = jnp.dot(normed_mlp_low, full_in, preferred_element_type=jnp.float32)

    def geglu(paired):
        return jax.nn.gelu(paired[:, :FF], approximate=False) * paired[:, FF:]

    hidden, geglu_back = jax.vjp(geglu, gate_up)
    hidden_low = hidden.astype(jnp.bfloat16)
    result = middle + jnp.dot(hidden_low, full_down, preferred_element_type=jnp.float32)
    grad_result = cotangent[0]
    grad_down_local = matmul_left(hidden_low, grad_result)
    grad_hidden = matmul_right(grad_result, full_down)
    grad_gate_up = geglu_back(grad_hidden)[0].astype(jnp.bfloat16)
    grad_in_local = matmul_left(normed_mlp_low, grad_gate_up)
    grad_normed_mlp = matmul_right(grad_gate_up, full_in)
    grad_middle_norm, grad_gain_second = mlp_norm_back(grad_normed_mlp)
    grad_middle = grad_result.astype(jnp.float32) + grad_middle_norm
    grad_branch = grad_middle.astype(jnp.bfloat16)
    grad_out_local = matmul_left(attended_low, grad_branch)
    grad_attended = matmul_right(grad_branch, full_out).astype(low)
    lanes = lax.axis_size("seq")
    if lanes == 8:
        gain_rows = jnp.pad(
            grad_gain_second.reshape(4, 1, held),
            ((0, 0), (0, PAD - 1), (held, D - 2 * held)),
        )
        hidden_rows = jnp.pad(
            hidden_low.T.reshape(4, owned_rows, count), ((0, 0), (0, PAD), (0, 0))
        )
        grad_qkv, grad_out, grad_in, grad_down, gain_sums, grad_normed = reduce_grads(
            [normed_low.T, attended_low.T, normed_mlp_low.T, hidden_rows.reshape(-1, count)],
            [grad_branch, grad_gate_up, grad_result],
            gain_rows.astype(jnp.bfloat16),
            [
                query_low, above, key_value, below, pos, grad_attended, logsum, cosine, sine,
                full_qkv, layer_norm(tokens, jnp.ones_like(gain_first)),
            ],
        )
        grad_tokens = grad_middle + norm_back(grad_normed)[0]
        return (
            result[None].astype(jnp.bfloat16),
            grad_tokens[None],
            grad_qkv,
            grad_out,
            grad_in,
            grad_down,
            gain_sums[0, :held],
            gain_sums[0, held : 2 * held],
        )
    grad_query, up, own, down = local_call(
        attend_back_kernel,
        [
            ((count, D), low),
            ((HALF_WINDOW, 2 * D), low),
            ((count, 2 * D), jnp.float32),
            ((HALF_WINDOW, 2 * D), low),
        ],
        query_low, above, key_value, below, pos, grad_attended, logsum, cosine, sine,
    )
    back_above, back_below = neighbours(up, down)
    (grad_mixed,) = local_call(
        join_kernel, [((count, 3 * D), low)], grad_query, own, back_above, back_below, cosine, sine
    )
    grad_qkv_local = matmul_left(normed_low, grad_mixed)
    grad_normed = matmul_right(grad_mixed, full_qkv)
    grad_tokens_norm, grad_gain_first = norm_back(grad_normed)
    grad_tokens = grad_middle + grad_tokens_norm
    owned = (
        lax.psum_scatter(
            grad_qkv_local.astype(jnp.bfloat16), "fsdp", scatter_dimension=0, tiled=True
        ).astype(jnp.float32),
        lax.psum_scatter(
            grad_out_local.astype(jnp.bfloat16), "fsdp", scatter_dimension=0, tiled=True
        ).astype(jnp.float32),
        lax.psum_scatter(
            grad_in_local.astype(jnp.bfloat16), "fsdp", scatter_dimension=0, tiled=True
        ).astype(jnp.float32),
        lax.psum_scatter(
            grad_down_local.astype(jnp.bfloat16), "fsdp", scatter_dimension=0, tiled=True
        ).astype(jnp.float32),
        lax.psum_scatter(
            grad_gain_first.astype(jnp.bfloat16), "fsdp", scatter_dimension=0, tiled=True
        ).astype(jnp.float32),
        lax.psum_scatter(
            grad_gain_second.astype(jnp.bfloat16), "fsdp", scatter_dimension=0, tiled=True
        ).astype(jnp.float32),
    )
    owned_flat = pack_rows(owned, 1)
    owned_share = owned_flat.shape[1] // lanes
    lane_part = lax.psum_scatter(
        owned_flat.reshape(lanes, owned_share), "seq", scatter_dimension=0, tiled=True
    )
    summed_row = (
        lax.all_gather(lane_part.astype(jnp.bfloat16), "seq", axis=0, tiled=True)
        .astype(lane_part.dtype)
        .reshape(-1)
    )
    grad_qkv, grad_out, grad_in, grad_down, grad_gain_attn, grad_gain_mlp = unpack_row(
        summed_row, owned, 1
    )
    return (
        result[None].astype(jnp.bfloat16),
        grad_tokens[None],
        grad_qkv,
        grad_out,
        grad_in,
        grad_down,
        grad_gain_attn,
        grad_gain_mlp,
    )


def solution(mesh):
    in_specs = (
        P("fsdp", "seq", None),
        P("fsdp", "seq"),
        P("fsdp", "seq", None),
        P("fsdp", None),
        P("fsdp", None),
        P("fsdp", None),
        P("fsdp", None),
        P("fsdp"),
        P("fsdp"),
    )
    out_specs = (
        P("fsdp", "seq", None),
        P("fsdp", "seq", None),
        P("fsdp", None),
        P("fsdp", None),
        P("fsdp", None),
        P("fsdp", None),
        P("fsdp"),
        P("fsdp"),
    )
    return jax.shard_map(
        on_device, mesh=mesh, in_specs=in_specs, out_specs=out_specs, check_vma=False
    )
```
